512 devices in a mesh: gx: 8 (over z_hi, y), gy: 4 (over x), shot: 16 (over z_lo, core).
Axes of the slice: x: 4, y: 4, z: 16 (z_hi: 2, z_lo: 8; z = z_hi * 8 + z_lo), core: 2. Of those that a mesh axis runs over, the one named last changes fastest.
Arguments:
- adj_prev: float32 [16, 256, 64, 256], P('shot', 'gx', 'gy'), may hold values from -6 to 6
- adj_cur: float32 [16, 256, 64, 256], P('shot', 'gx', 'gy'), may hold values from -6 to 6
- fwd_accel: bfloat16 [16, 4, 256, 64, 256], P('shot', None, 'gx', 'gy'), may hold values from -6 to 6
- courant2: float32 [256, 64, 256], P('gx', 'gy'), may hold values from 0.05 to 0.18
- traces: bfloat16 [16, 4, 2048], P('shot', None, ('gx', 'gy')), may hold values from -6 to 6
- weights: bfloat16 [8, 4, 64, 16, 256], P('gx', 'gy'), may hold values from -3 to 3
- rblock: int32 [8, 4, 64], P('gx', 'gy'), may hold values from 0 to 127
- column: int32 [8, 4, 64], P('gx', 'gy'), may hold values from 0 to 511
- counts: int32 [8, 4], P('gx', 'gy'), may hold values from 16 to 64
Outputs:
- adj_prev_out: float32 [16, 256, 64, 256], P('shot', 'gx', 'gy')
- adj_cur_out: float32 [16, 256, 64, 256], P('shot', 'gx', 'gy')
- gradient: float32 [128, 32, 128], P('gx', 'gy')
The draws below stay inside these ranges and needn't reach their ends.
All inputs are finite; a program needn't handle non-finite values.
Results may differ from the reference program's by a relative error of at most 0.00045.
Values may be sent and summed in bfloat16 or wider, within the bound.
A program may use at most 128 MiB of HBM per device.

```python
import jax
import jax.numpy as jnp
from jax import lax

CX = 32
CY = 16
NZ = 256
STEPS = 4
SLOTS = 64
RB = 16
TX = 8
TY = 4
SHOTS = 16
NX = 256
NY = 64
NREC = 2048


def draw_counts(key, part):
    tiles = TX * TY
    drawn = jax.random.randint(key, (tiles,), SLOTS // 4, SLOTS + 1)
    chosen = jax.random.randint(jax.random.fold_in(key, 7), (), 0, tiles)
    drawn = jnp.where(jnp.arange(tiles) == chosen, SLOTS, drawn)
    return drawn.reshape(TX, TY).astype(jnp.int32)


def set_ends(values, stream_key, smallest, largest):
    spot = [jax.random.randint(jax.random.fold_in(stream_key, axis), (), 0, length) for axis, length in enumerate(values.shape)]
    longest = values.shape.index(max(values.shape))
    neighbour = spot[:longest] + [(spot[longest] + 1) % values.shape[longest]] + spot[longest + 1:]
    return values.at[tuple(spot)].set(smallest).at[tuple(neighbour)].set(largest)


def block_levels(stream_key, dims, pieces, least, high):
    def one(axis_at, shards_of):
        steps = jax.random.uniform(jax.random.fold_in(jax.random.fold_in(stream_key, 6), axis_at), (shards_of,), jnp.float32, least / len(pieces), high / len(pieces))
        return jnp.repeat(jnp.exp(steps), dims[axis_at] // shards_of).reshape((-1,) + (1,) * (len(dims) - axis_at - 1))

    level = one(*pieces[0])
    for cut in pieces[1:]:
        level = level * one(*cut)
    return level


def centred(key, extent, deviation, most, split=(), held_as=jnp.bfloat16):
    array = jax.random.normal(key, extent, jnp.float32) * deviation
    if len(split) > 0:
        array = block_levels(key, extent, split, -0.22, 0.18) * array
    return jnp.clip(array, min=-most, max=most).astype(held_as)


def setup_inputs(seed: int = 0) -> dict:
    key_list = jax.random.split(jax.random.key(seed), 10)
    adj_prev = centred(key_list[0], (SHOTS, NX, NY, NZ), 1.0, 6.0, ((0, 16), (1, 8), (2, 4)), jnp.float32)
    adj_cur = centred(key_list[1], (SHOTS, NX, NY, NZ), 1.0, 6.0, ((0, 16), (1, 8), (2, 4)), jnp.float32)
    fwd_accel = centred(key_list[2], (SHOTS, STEPS, NX, NY, NZ), 1.0, 6.0, ((0, 16), (2, 8), (3, 4)))
    courant2 = jnp.clip(0.05 + 0.13000001 * jax.random.uniform(key_list[3], (NX, NY, NZ), jnp.float32) ** block_levels(key_list[3], (NX, NY, NZ), ((0, 8), (1, 4)), -0.2, 0.2), 0.05, 0.18)
    traces = centred(key_list[4], (SHOTS, STEPS, NREC), 1.0, 6.0, ((0, 16), (2, 32)))
    weights = centred(key_list[5], (TX, TY, SLOTS, RB, NZ), 0.5, 3.0, ((0, 8), (1, 4)))
    rblock = set_ends(jax.random.randint(key_list[6], (TX, TY, SLOTS), 0, NREC // RB), jax.random.fold_in(key_list[6], 1), 0, (NREC // RB) - 1).astype(jnp.int32)
    column = set_ends(jax.random.randint(key_list[7], (TX, TY, SLOTS), 0, CX * CY), jax.random.fold_in(key_list[7], 1), 0, (CX * CY) - 1).astype(jnp.int32)
    counts = draw_counts(jax.random.fold_in(key_list[9], 71), 0)
    return dict(adj_prev=adj_prev, adj_cur=adj_cur, fwd_accel=fwd_accel, courant2=courant2, traces=traces, weights=weights, rblock=rblock, column=column, counts=counts)


LAPLACE_COEFS = (-205.0 / 72.0, 8.0 / 5.0, -1.0 / 5.0, 8.0 / 315.0, -1.0 / 560.0)


def laplace(field):
    padded = jnp.pad(field, 4)
    size_x, size_y, size_z = field.shape
    center = padded[4:4 + size_x, 4:4 + size_y, 4:4 + size_z]
    total = 3.0 * LAPLACE_COEFS[0] * center
    for offset in range(1, 5):
        weight = LAPLACE_COEFS[offset]
        total = total + weight * (padded[4 + offset:4 + offset + size_x, 4:4 + size_y, 4:4 + size_z] + padded[4 - offset:4 - offset + size_x, 4:4 + size_y, 4:4 + size_z])
        total = total + weight * (padded[4:4 + size_x, 4 + offset:4 + offset + size_y, 4:4 + size_z] + padded[4:4 + size_x, 4 - offset:4 - offset + size_y, 4:4 + size_z])
        total = total + weight * (padded[4:4 + size_x, 4:4 + size_y, 4 + offset:4 + offset + size_z] + padded[4:4 + size_x, 4:4 + size_y, 4 - offset:4 - offset + size_z])
    return total


def restrict(fine):
    size_x, size_y, size_z = fine.shape
    return fine.reshape(size_x // 2, 2, size_y // 2, 2, size_z // 2, 2).mean(axis=(1, 3, 5))


def reference(adj_prev, adj_cur, fwd_accel, courant2, traces, weights, rblock, column, counts):
    tiles_x, tiles_y = counts.shape
    slots = rblock.shape[2]
    recv_block = weights.shape[3]
    live_slots = (jnp.arange(slots, dtype=jnp.int32)[None, None, :] < counts[:, :, None]).astype(jnp.float32)
    onehot = (column[..., None] == jnp.arange(CX * CY, dtype=jnp.int32)).astype(jnp.float32) * live_slots[..., None]
    weights_wide = weights.astype(jnp.float32)

    def one_shot(shot_data):
        previous, current, accel, trace = shot_data
        blocks = trace.reshape(STEPS, -1, recv_block)
        picked = blocks[:, rblock].astype(jnp.float32)
        contrib = jnp.einsum("tabsr,absrz->tabsz", picked, weights_wide, precision=lax.Precision.HIGHEST)
        source = jnp.einsum("absc,tabsz->tabcz", onehot, contrib, precision=lax.Precision.HIGHEST)
        source = source.reshape(STEPS, tiles_x, tiles_y, CX, CY, NZ).transpose(0, 1, 3, 2, 4, 5).reshape(STEPS, tiles_x * CX, tiles_y * CY, NZ)
        fine = jnp.zeros(current.shape, jnp.float32)
        for step_index in range(STEPS):
            next_field = 2.0 * current - previous + courant2 * laplace(current) + source[step_index]
            fine = fine + accel[step_index].astype(jnp.float32) * next_field
            previous, current = current, next_field
        return previous, current, restrict(fine)

    outputs = lax.map(one_shot, (adj_prev, adj_cur, fwd_accel, traces))
    return outputs[0], outputs[1], jnp.sum(outputs[2], axis=0)
```

```python
import functools

import jax
import jax.numpy as jnp
import ml_dtypes
from jax import lax
from jax.experimental import pallas as pl
from jax.experimental.pallas import tpu as pltpu
from jax.sharding import PartitionSpec as P

MESH = pl.DeviceIdType.MESH
COEFS = (-205.0 / 72.0, 8.0 / 5.0, -1.0 / 5.0, 8.0 / 315.0, -1.0 / 560.0)
F32, BF16, I32 = jnp.float32, jnp.bfloat16, jnp.int32
STEPS, CX, CY, HALF = 4, 32, 16, 128
SLOTS, RB = 64, 16
GX, GY, SHOTS = 8, 4, 16
LO, HI = 0, 1


def iota(shape, dim):
    return lax.broadcasted_iota(I32, shape, dim)


def flag(condition):
    return jnp.where(condition, 1.0, 0.0).astype(F32)


def kernel(
    prev_h, cur_h, acc_h, c2_h, w_h, tr_ref, rb_ref, col_ref, cnt_ref,
    prev_o, cur_o, grad_o,
    field, prev, accel, c2, weights, base, source, fine, packed, band_hi, band_lo,
    halo_y_lo, halo_y_hi, halo_x, send_x, traces, block, spread, onehot, pick, pooled, local, arrived, total,
    in_sem, out_sem, xs_sem, xr_sem, ys_sem, yr_sem, ts_sem, tr_sem, rs_sem, rr_sem, as_sem, ar_sem,
):
    gx, gy, shot = lax.axis_index("gx"), lax.axis_index("gy"), lax.axis_index("shot")
    tile = gx * GY + gy

    def tile_peer(i):
        other = lax.rem(tile + i, GX * GY)
        return {"gx": lax.div(other, GY), "gy": lax.rem(other, GY)}, other

    def shot_peer(i):
        other = lax.rem(shot + i, SHOTS)
        return {"shot": other}, other

    loads = []
    for half in range(2):
        lanes = pl.ds(half * HALF, HALF)
        loads.append(pltpu.make_async_copy(
            cur_h.at[:, :, lanes], field.at[0, half, pl.ds(4, CX), pl.ds(8, CY), :], in_sem.at[half]))
        loads.append(pltpu.make_async_copy(prev_h.at[:, :, lanes], prev.at[half], in_sem.at[2 + half]))
        loads.append(pltpu.make_async_copy(c2_h.at[:, :, lanes], c2.at[half], in_sem.at[4 + half]))
        loads.append(pltpu.make_async_copy(acc_h.at[:, :, :, lanes], accel.at[:, half], in_sem.at[6 + half]))
    loads.append(pltpu.make_async_copy(w_h, weights, in_sem.at[8]))
    for copy in loads:
        copy.start()

    barrier = pltpu.get_barrier_semaphore()

    def greet_tile(i, carry):
        pl.semaphore_signal(barrier, 1, device_id=tile_peer(i)[0], device_id_type=MESH)
        return carry

    def greet_shot(i, carry):
        pl.semaphore_signal(barrier, 1, device_id=shot_peer(i)[0], device_id_type=MESH)
        return carry

    lax.fori_loop(1, GX * GY, greet_tile, 0)
    lax.fori_loop(1, SHOTS, greet_shot, 0)

    zero_rows = jnp.zeros((CX, 8, HALF), F32)
    zero_planes = jnp.zeros((4, 32, HALF), F32)
    for t in range(STEPS):
        for half in range(2):
            field[t, half, pl.ds(0, 4), :, :] = zero_planes
            field[t, half, pl.ds(4 + CX, 4), :, :] = zero_planes
            field[t, half, pl.ds(4, CX), pl.ds(0, 8), :] = zero_rows
            field[t, half, pl.ds(4, CX), pl.ds(24, 8), :] = zero_rows
            halo_y_lo[t, half, :, pl.ds(8, 8), :] = zero_rows
            halo_y_hi[t, half, :, pl.ds(0, 8), :] = zero_rows

    @pl.when(gx == 0)
    def _():
        halo_x[:, LO] = jnp.zeros((STEPS, 2, 5, CY, HALF), BF16)

    @pl.when(gx == GX - 1)
    def _():
        halo_x[:, HI] = jnp.zeros((STEPS, 2, 5, CY, HALF), BF16)

    @pl.when(gy == 0)
    def _():
        for t in range(STEPS):
            for half in range(2):
                halo_y_lo[t, half, :, pl.ds(0, 8), :] = zero_rows

    @pl.when(gy == GY - 1)
    def _():
        for t in range(STEPS):
            for half in range(2):
                halo_y_hi[t, half, :, pl.ds(8, 8), :] = zero_rows

    block[...] = jnp.zeros((8, HALF), F32)
    block[pl.ds(0, STEPS), pl.ds(0, 64)] = tr_ref[0].astype(F32)
    as_is = block[...]
    turned = pltpu.roll(as_is, 64, 1)
    traces[tile, pl.ds(0, 1), :] = as_is[0:1] + turned[1:2]
    traces[tile, pl.ds(1, 1), :] = as_is[2:3] + turned[3:4]

    distance = jnp.abs(iota((256, 256), 0) - iota((256, 256), 1))
    band = jnp.zeros((256, 256), F32)
    rest = jnp.zeros((256, 256), F32)
    for k in range(1, 5):
        high = float(ml_dtypes.bfloat16(COEFS[k]))
        band = jnp.where(distance == k, high, band)
        rest = jnp.where(distance == k, COEFS[k] - high, rest)
    band_hi[pl.ds(0, 256), :] = band.astype(BF16)
    band_hi[pl.ds(256, 256), :] = band.astype(BF16)
    band_lo[...] = rest.astype(BF16)

    spread[...] = flag((iota((128, 1024), 0) & 15) == (iota((128, 1024), 1) & 15)).astype(BF16)
    slot_row = iota((1, SLOTS), 1)
    live = slot_row < cnt_ref[...]
    hit = flag((iota((CX * CY, SLOTS), 0) == col_ref[...]) & live).astype(BF16)
    onehot[...] = jnp.concatenate([hit, hit], axis=1)
    diagonal = iota((SLOTS, SLOTS), 0) == iota((SLOTS, SLOTS), 1)
    rb_column = jnp.sum(jnp.where(diagonal, rb_ref[...].astype(F32), 0.0), axis=1, keepdims=True).astype(I32)
    pick[...] = flag((rb_column >> 2) == iota((SLOTS, 32), 1))
    quarter = rb_column & 3

    for copy in loads[0:8:4]:
        copy.wait()

    def pack_edge(t, half, x, value):
        high = value.astype(BF16)
        if x < 4:
            send_x[t, LO, half, x] = high
            if x == 0:
                send_x[t, LO, half, 4] = (value - high.astype(F32)).astype(BF16)
        if x >= CX - 4:
            send_x[t, HI, half, x - (CX - 4)] = high
            if x == CX - 1:
                send_x[t, HI, half, 4] = (value - high.astype(F32)).astype(BF16)

    def split(half, x, value):
        high = value.astype(BF16)
        packed[x, :, pl.ds(half * HALF, HALF)] = high
        packed[x, :, pl.ds(256 + half * HALF, HALF)] = (value - high.astype(F32)).astype(BF16)

    def x_copy(t, side):
        return pltpu.make_async_remote_copy(
            src_ref=send_x.at[t, 1 - side], dst_ref=halo_x.at[t, side],
            send_sem=xs_sem.at[t, side], recv_sem=xr_sem.at[t, side],
            device_id={"gx": gx + 1 if side == LO else gx - 1}, device_id_type=MESH)

    def y_copy(t, side):
        if side == LO:
            src = field.at[t, :, pl.ds(4, CX), pl.ds(20, 4), :]
            dst = halo_y_lo.at[t, :, :, pl.ds(4, 4), :]
        else:
            src = field.at[t, :, pl.ds(4, CX), pl.ds(8, 4), :]
            dst = halo_y_hi.at[t, :, :, pl.ds(8, 4), :]
        return pltpu.make_async_remote_copy(
            src_ref=src, dst_ref=dst, send_sem=ys_sem.at[t, side], recv_sem=yr_sem.at[t, side],
            device_id={"gy": gy + 1 if side == LO else gy - 1}, device_id_type=MESH)

    sends_x = {LO: gx < GX - 1, HI: gx > 0}
    gets_x = {LO: gx > 0, HI: gx < GX - 1}
    sends_y = {LO: gy < GY - 1, HI: gy > 0}
    gets_y = {LO: gy > 0, HI: gy < GY - 1}

    def each(conditions, make, t, act):
        for side in (LO, HI):
            @pl.when(conditions[side])
            def _():
                getattr(make(t, side), act)()

    EDGES = (0, 1, 2, 3, CX - 4, CX - 3, CX - 2, CX - 1)
    for half in range(2):
        for x in EDGES:
            pack_edge(0, half, x, field[0, half, 4 + x, pl.ds(8, CY), :])

    pl.semaphore_wait(barrier, GX * GY - 1 + SHOTS - 1)

    each(sends_x, x_copy, 0, "start")

    def trace_copy(i):
        peer, _ = tile_peer(i)
        return pltpu.make_async_remote_copy(
            src_ref=traces.at[tile, pl.ds(0, 2)], dst_ref=traces.at[tile, pl.ds(0, 2)],
            send_sem=ts_sem.at[i], recv_sem=tr_sem.at[tile], device_id=peer, device_id_type=MESH)

    def start_trace(i, carry):
        trace_copy(i).start()
        return carry

    lax.fori_loop(1, GX * GY, start_trace, 0)
    each(sends_y, y_copy, 0, "start")

    def split_plane(x, carry):
        for half in range(2):
            split(half, x, field[0, half, 4 + x, pl.ds(8, CY), :])
        return carry

    lax.fori_loop(0, CX, split_plane, 0)
    for i in (1, 2, 3, 5, 6, 7, 8):
        loads[i].wait()

    def base_step(t):
        def chunk(c, carry):
            x0 = pl.multiple_of(c * 8, 8)
            both = packed[pl.ds(x0, 8)].reshape(128, 512)
            along_z = jnp.dot(both, band_hi[...], preferred_element_type=F32)
            along_z += jnp.dot(both[:, :256], band_lo[...], preferred_element_type=F32)
            for half in range(2):
                planes = [field[t, half, x0 + j, pl.ds(8, CY), :] for j in range(16)]
                for i in range(8):
                    center = planes[i + 4]
                    lap = along_z[i * CY : (i + 1) * CY, half * HALF : (half + 1) * HALF] + (3.0 * COEFS[0]) * center
                    for k in range(1, 5):
                        lap += COEFS[k] * (
                            (planes[i + 4 - k] + planes[i + 4 + k])
                            + (field[t, half, x0 + 4 + i, pl.ds(8 - k, CY), :] + field[t, half, x0 + 4 + i, pl.ds(8 + k, CY), :]))
                    if t == 0:
                        before = prev[half, x0 + i]
                    else:
                        before = field[t - 1, half, x0 + 4 + i, pl.ds(8, CY), :] - source[t, half, x0 + i]
                    base[half, x0 + i] = 2.0 * center - before + c2[half, x0 + i] * lap
            return carry

        lax.fori_loop(0, CX // 8, chunk, 0)

    def fix_plane(t, half, x, across):
        low = high = None
        for k in range(1, 5):
            a = COEFS[k] * halo_y_lo[t, half, x, pl.ds(8 - k, 8), :]
            b = COEFS[k] * halo_y_hi[t, half, x, pl.ds(k, 8), :]
            low, high = (a, b) if low is None else (low + a, high + b)
        lap = jnp.concatenate([low, high], axis=0)
        if across is not None:
            lap += across
        value = base[half, x] + c2[half, x] * lap
        if t == 0:
            value += source[0, half, x]
        field[t + 1, half, 4 + x, pl.ds(8, CY), :] = value
        if t < STEPS - 1:
            split(half, x, value)
        product = accel[t, half, x].astype(F32) * value
        fine[half, x] = product if t == 0 else fine[half, x] + product
        return value

    def fix_edges(t, side):
        for half in range(2):
            layer = [halo_x[t, side, half, j].astype(F32) for j in range(4)]
            near = 3 if side == LO else 0
            layer[near] += halo_x[t, side, half, 4].astype(F32)
            for j in range(4):
                x = j if side == LO else CX - 1 - j
                across = None
                for k in range(j + 1, 5):
                    away = k - j - 1
                    term = COEFS[k] * layer[3 - away if side == LO else away]
                    across = term if across is None else across + term
                value = fix_plane(t, half, x, across)
                if t < STEPS - 1:
                    pack_edge(t + 1, half, x, value)

    def fix_middle(t):
        def plane(x, carry):
            for half in range(2):
                fix_plane(t, half, x, None)
            return carry

        lax.fori_loop(4, CX - 4, plane, 0)

    def make_source(t):
        row, odd = t // 2, t % 2
        rows = traces[:, row, :]
        got = jnp.dot(pick[...].astype(BF16), rows.astype(BF16), preferred_element_type=F32)
        lane = iota((SLOTS, HALF), 1)
        keep = ((lane >> 6) == odd) & (((lane >> 4) & 3) == quarter)
        got = jnp.where(keep, got, 0.0).astype(BF16)
        wide = jnp.dot(got, spread[...], preferred_element_type=F32)
        own = (iota((SLOTS, 1024), 1) >> 4) == iota((SLOTS, 1024), 0)
        wide = jnp.where(own, wide, 0.0).astype(BF16)
        contribution = jnp.dot(wide, weights[...], preferred_element_type=F32)
        high = contribution.astype(BF16)
        low = (contribution - high.astype(F32)).astype(BF16)
        stacked = jnp.concatenate([high, low], axis=0)
        dense = jnp.dot(onehot[...], stacked, preferred_element_type=F32)
        for half in range(2):
            source[t, half] = dense[:, half * HALF : (half + 1) * HALF].reshape(CX, CY, HALF)

    base_step(0)

    def wait_trace(i, carry):
        _, other = tile_peer(i)
        pltpu.make_async_remote_copy(
            src_ref=traces.at[other, pl.ds(0, 2)], dst_ref=traces.at[other, pl.ds(0, 2)],
            send_sem=ts_sem.at[i], recv_sem=tr_sem.at[other], device_id=tile_peer(i)[0], device_id_type=MESH).wait_recv()
        return carry

    lax.fori_loop(1, GX * GY, wait_trace, 0)
    make_source(0)

    for t in range(STEPS):
        each(gets_y, y_copy, t, "wait_recv")
        each(gets_x, x_copy, t, "wait_recv")
        fix_edges(t, LO)
        fix_edges(t, HI)
        if t < STEPS - 1:
            each(sends_x, x_copy, t + 1, "start")
        fix_middle(t)
        if t < STEPS - 1:
            each(sends_y, y_copy, t + 1, "start")
            make_source(t + 1)
            base_step(t + 1)

    outs = []
    for half in range(2):
        lanes = pl.ds(half * HALF, HALF)
        for n, (t, out) in enumerate(((STEPS - 1, prev_o), (STEPS, cur_o))):
            outs.append(pltpu.make_async_copy(
                field.at[t, half, pl.ds(4, CX), pl.ds(8, CY), :], out.at[:, :, lanes], out_sem.at[2 * half + n]))
    for copy in outs:
        copy.start()

    pairs = [(fine[half].reshape(CX // 2, 2, CY, HALF)) for half in range(2)]
    pairs = [(p[:, 0] + p[:, 1]).reshape(CX // 2 * CY, HALF) for p in pairs]
    both = jnp.concatenate(pairs, axis=1)
    pool = (flag((iota((256, 128), 0) >> 1) == iota((256, 128), 1)) * 0.125).astype(BF16)
    high = both.astype(BF16)
    left = both - high.astype(F32)
    mid = left.astype(BF16)
    last = (left - mid.astype(F32)).astype(BF16)
    pooled[...] = (
        jnp.dot(high, pool, preferred_element_type=F32)
        + jnp.dot(mid, pool, preferred_element_type=F32)
        + jnp.dot(last, pool, preferred_element_type=F32))
    coarse = pooled[pl.ds(0, 128, stride=2), :] + pooled[pl.ds(1, 128, stride=2), :]
    local[...] = coarse.reshape(CX // 2, 8, HALF)

    def row_copy(i, index_of_peer=False):
        peer, other = shot_peer(i)
        return pltpu.make_async_remote_copy(
            src_ref=local.at[other], dst_ref=arrived.at[shot],
            send_sem=rs_sem.at[i], recv_sem=rr_sem.at[shot], device_id=peer, device_id_type=MESH)

    def start_row(i, carry):
        row_copy(i).start()
        return carry

    lax.fori_loop(1, SHOTS, start_row, 0)
    arrived[shot] = local[shot]

    def wait_row(i, carry):
        peer, other = shot_peer(i)
        pltpu.make_async_remote_copy(
            src_ref=local.at[other], dst_ref=arrived.at[other],
            send_sem=rs_sem.at[i], recv_sem=rr_sem.at[other], device_id=peer, device_id_type=MESH).wait_recv()
        return carry

    lax.fori_loop(1, SHOTS, wait_row, 0)
    total[shot] = jnp.sum(arrived[...], axis=0)

    def sum_copy(i):
        peer, _ = shot_peer(i)
        return pltpu.make_async_remote_copy(
            src_ref=total.at[shot], dst_ref=total.at[shot],
            send_sem=as_sem.at[i], recv_sem=ar_sem.at[shot], device_id=peer, device_id_type=MESH)

    def start_sum(i, carry):
        sum_copy(i).start()
        return carry

    lax.fori_loop(1, SHOTS, start_sum, 0)

    def end_trace(i, carry):
        trace_copy(i).wait_send()
        return carry

    lax.fori_loop(1, GX * GY, end_trace, 0)
    for t in range(STEPS):
        each(sends_x, x_copy, t, "wait_send")
        each(sends_y, y_copy, t, "wait_send")

    def wait_sum(i, carry):
        peer, other = shot_peer(i)
        pltpu.make_async_remote_copy(
            src_ref=total.at[other], dst_ref=total.at[other],
            send_sem=as_sem.at[i], recv_sem=ar_sem.at[other], device_id=peer, device_id_type=MESH).wait_recv()
        return carry

    lax.fori_loop(1, SHOTS, wait_sum, 0)
    last_copy = pltpu.make_async_copy(total, grad_o, out_sem.at[4])
    last_copy.start()

    def end_rows(i, carry):
        row_copy(i).wait_send()
        sum_copy(i).wait_send()
        return carry

    lax.fori_loop(1, SHOTS, end_rows, 0)
    for copy in outs:
        copy.wait()
    last_copy.wait()


def local_part(adj_prev, adj_cur, fwd_accel, courant2, traces, weights, rblock, column, counts):
    tile = (CX, CY, 2 * HALF)
    any_ = pl.BlockSpec(memory_space=pl.ANY)
    vmem = pl.BlockSpec(memory_space=pltpu.VMEM)
    dma = pltpu.SemaphoreType.DMA
    previous, current, gradient = pl.pallas_call(
        kernel,
        out_shape=(
            jax.ShapeDtypeStruct(tile, F32),
            jax.ShapeDtypeStruct(tile, F32),
            jax.ShapeDtypeStruct((CX // 2, CY // 2, HALF), F32),
        ),
        in_specs=[any_] * 5 + [vmem] * 4,
        out_specs=(any_, any_, any_),
        scratch_shapes=[
            pltpu.VMEM((STEPS + 1, 2, CX + 8, 32, HALF), F32),
            pltpu.VMEM((2, CX, CY, HALF), F32),
            pltpu.VMEM((STEPS, 2, CX, CY, HALF), BF16),
            pltpu.VMEM((2, CX, CY, HALF), F32),
            pltpu.VMEM((SLOTS * RB, 256), BF16),
            pltpu.VMEM((2, CX, CY, HALF), F32),
            pltpu.VMEM((STEPS, 2, CX, CY, HALF), F32),
            pltpu.VMEM((2, CX, CY, HALF), F32),
            pltpu.VMEM((CX, CY, 512), BF16),
            pltpu.VMEM((512, 256), BF16),
            pltpu.VMEM((256, 256), BF16),
            pltpu.VMEM((STEPS, 2, CX, 16, HALF), F32),
            pltpu.VMEM((STEPS, 2, CX, 16, HALF), F32),
            pltpu.VMEM((STEPS, 2, 2, 5, CY, HALF), BF16),
            pltpu.VMEM((STEPS, 2, 2, 5, CY, HALF), BF16),
            pltpu.VMEM((GX * GY, 8, HALF), F32),
            pltpu.VMEM((8, HALF), F32),
            pltpu.VMEM((128, 1024), BF16),
            pltpu.VMEM((CX * CY, 2 * SLOTS), BF16),
            pltpu.VMEM((SLOTS, 32), F32),
            pltpu.VMEM((256, HALF), F32),
            pltpu.VMEM((CX // 2, 8, HALF), F32),
            pltpu.VMEM((SHOTS, 8, HALF), F32),
            pltpu.VMEM((CX // 2, 8, HALF), F32),
            dma((9,)), dma((5,)),
            dma((STEPS, 2)), dma((STEPS, 2)), dma((STEPS, 2)), dma((STEPS, 2)),
            dma((GX * GY,)), dma((GX * GY,)),
            dma((SHOTS,)), dma((SHOTS,)), dma((SHOTS,)), dma((SHOTS,)),
        ],
        compiler_params=pltpu.CompilerParams(
            collective_id=0, has_side_effects=True, vmem_limit_bytes=48 << 20),
    )(
        adj_prev[0], adj_cur[0], fwd_accel[0], courant2, weights[0, 0].reshape(SLOTS * RB, 256),
        traces, rblock[0], column[0], counts,
    )
    return previous[None], current[None], gradient


def solution(mesh):
    return jax.shard_map(
        local_part,
        mesh=mesh,
        in_specs=(
            P("shot", "gx", "gy", None),
            P("shot", "gx", "gy", None),
            P("shot", None, "gx", "gy", None),
            P("gx", "gy", None),
            P("shot", None, ("gx", "gy")),
            P("gx", "gy", None, None, None),
            P("gx", "gy", None),
            P("gx", "gy", None),
            P("gx", "gy"),
        ),
        out_specs=(P("shot", "gx", "gy", None), P("shot", "gx", "gy", None), P("gx", "gy", None)),
        check_vma=False,
    )
```

```python
import functools

import jax
import jax.numpy as jnp
import ml_dtypes
from jax import lax
from jax.experimental import pallas as pl
from jax.experimental.pallas import tpu as pltpu
from jax.sharding import PartitionSpec as P

MESH = pl.DeviceIdType.MESH
COEFS = (-205.0 / 72.0, 8.0 / 5.0, -1.0 / 5.0, 8.0 / 315.0, -1.0 / 560.0)
F32, BF16, I32 = jnp.float32, jnp.bfloat16, jnp.int32
STEPS, CX, CY, HALF = 4, 32, 16, 128
SLOTS, RB = 64, 16
GX, GY, SHOTS = 8, 4, 16
LO, HI = 0, 1
PARTS = 4


def iota(shape, dim):
    return lax.broadcasted_iota(I32, shape, dim)


def flag(condition):
    return jnp.where(condition, 1.0, 0.0).astype(F32)


def kernel(
    prev_h, cur_h, acc_h, c2_h, w_h, tr_h, rb_h, col_h, cnt_h,
    prev_o, cur_o, grad_o,
    field, prev, accel, c2, weights, tr_ref, rb_ref, col_ref, cnt_ref,
    base, source, fine, packed, band_hi, band_lo, halo_y_lo, halo_y_hi, halo_x, send_x,
    traces, block, spread, onehot, pick, pooled, local, arrived, arrived_edge, total, final,
    in_sem, xs_sem, xr_sem, ys_sem, yr_sem, zs_sem, zr_sem, ts_sem, tr_sem, rs_sem, rr_sem, es_sem, er_sem, as_sem, ar_sem, bs_sem, out_sem,
):
    gx, gy, shot = lax.axis_index("gx"), lax.axis_index("gy"), lax.axis_index("shot")
    z_hi, row = lax.div(gx, 4), lax.rem(gx, 4)
    spot = row * 4 + gy

    def spot_peer(i):
        other = lax.rem(spot + i, 16)
        return {"gx": z_hi * 4 + lax.div(other, 4), "gy": lax.rem(other, 4)}, other

    partner = {"gx": lax.rem(gx + 4, GX)}
    faces_half = (gx == 3) | (gx == 4)

    def shot_peer(i):
        other = lax.rem(shot + i, SHOTS)
        return {"shot": other}, other

    barrier = pltpu.get_barrier_semaphore()

    def greet(device):
        pl.semaphore_signal(barrier, 1, device_id=device, device_id_type=MESH)

    greet(partner)

    @pl.when(faces_half)
    def _():
        greet({"gx": 7 - gx})

    def greet_shot(i, carry):
        greet(shot_peer(i)[0])
        return carry

    def greet_spot(i, carry):
        greet(spot_peer(i)[0])
        return carry

    lax.fori_loop(1, SHOTS, greet_shot, 0)
    lax.fori_loop(1, 16, greet_spot, 0)

    loads = []
    for half in range(2):
        lanes = pl.ds(half * HALF, HALF)
        loads.append(pltpu.make_async_copy(
            cur_h.at[:, :, lanes], field.at[0, half, pl.ds(4, CX), pl.ds(8, CY), :], in_sem.at[half]))
        loads.append(pltpu.make_async_copy(prev_h.at[:, :, lanes], prev.at[half], in_sem.at[2 + half]))
        loads.append(pltpu.make_async_copy(c2_h.at[:, :, lanes], c2.at[half], in_sem.at[4 + half]))
        loads.append(pltpu.make_async_copy(acc_h.at[:, :, :, lanes], accel.at[:, half], in_sem.at[6 + half]))
    loads.append(pltpu.make_async_copy(w_h, weights, in_sem.at[8]))
    for n, (src, dst) in enumerate(((tr_h, tr_ref), (rb_h, rb_ref), (col_h, col_ref), (cnt_h, cnt_ref))):
        loads.append(pltpu.make_async_copy(src, dst, in_sem.at[9 + n]))
    for copy in loads:
        copy.start()

    zero_rows = jnp.zeros((CX, 8, HALF), F32)
    zero_planes = jnp.zeros((4, 32, HALF), F32)
    for t in range(STEPS):
        for half in range(2):
            field[t, half, pl.ds(0, 4), :, :] = zero_planes
            field[t, half, pl.ds(4 + CX, 4), :, :] = zero_planes
            field[t, half, pl.ds(4, CX), pl.ds(0, 8), :] = zero_rows
            field[t, half, pl.ds(4, CX), pl.ds(24, 8), :] = zero_rows
            halo_y_lo[t, half, :, pl.ds(8, 8), :] = zero_rows
            halo_y_hi[t, half, :, pl.ds(0, 8), :] = zero_rows

    @pl.when(gx == 0)
    def _():
        halo_x[:, LO] = jnp.zeros((STEPS, 2, 5, CY, HALF), BF16)

    @pl.when(gx == GX - 1)
    def _():
        halo_x[:, HI] = jnp.zeros((STEPS, 2, 5, CY, HALF), BF16)

    @pl.when(gy == 0)
    def _():
        for t in range(STEPS):
            for half in range(2):
                halo_y_lo[t, half, :, pl.ds(0, 8), :] = zero_rows

    @pl.when(gy == GY - 1)
    def _():
        for t in range(STEPS):
            for half in range(2):
                halo_y_hi[t, half, :, pl.ds(8, 8), :] = zero_rows

    for copy in loads[9:]:
        copy.wait()

    block[...] = jnp.zeros((8, HALF), F32)
    block[pl.ds(0, STEPS), pl.ds(0, 64)] = tr_ref[0].astype(F32)
    as_is = block[...]
    turned = pltpu.roll(as_is, 64, 1)
    traces[spot, z_hi, pl.ds(0, 1), :] = as_is[0:1] + turned[1:2]
    traces[spot, z_hi, pl.ds(1, 1), :] = as_is[2:3] + turned[3:4]

    distance = jnp.abs(iota((256, 256), 0) - iota((256, 256), 1))
    band = jnp.zeros((256, 256), F32)
    rest = jnp.zeros((256, 256), F32)
    for k in range(1, 5):
        high = float(ml_dtypes.bfloat16(COEFS[k]))
        band = jnp.where(distance == k, high, band)
        rest = jnp.where(distance == k, COEFS[k] - high, rest)
    band_hi[pl.ds(0, 256), :] = band.astype(BF16)
    band_hi[pl.ds(256, 256), :] = band.astype(BF16)
    band_lo[...] = rest.astype(BF16)

    spread[...] = flag((iota((128, 1024), 0) & 15) == (iota((128, 1024), 1) & 15)).astype(BF16)
    slot_row = iota((1, SLOTS), 1)
    live = slot_row < cnt_ref[...]
    hit = flag((iota((CX * CY, SLOTS), 0) == col_ref[...]) & live).astype(BF16)
    onehot[...] = jnp.concatenate([hit, hit], axis=1)
    diagonal = iota((SLOTS, SLOTS), 0) == iota((SLOTS, SLOTS), 1)
    rb_column = jnp.sum(jnp.where(diagonal, rb_ref[...].astype(F32), 0.0), axis=1, keepdims=True).astype(I32)
    holder = rb_column >> 2
    pick[...] = flag(((holder & 15) * 2 + (holder >> 4)) == iota((SLOTS, 32), 1))
    quarter = rb_column & 3

    for copy in loads[0:8:4]:
        copy.wait()

    def pack_edge(t, half, x, value):
        high = value.astype(BF16)
        if x < 4:
            send_x[t, LO, half, x] = high
            if x == 0:
                send_x[t, LO, half, 4] = (value - high.astype(F32)).astype(BF16)
        if x >= CX - 4:
            send_x[t, HI, half, x - (CX - 4)] = high
            if x == CX - 1:
                send_x[t, HI, half, 4] = (value - high.astype(F32)).astype(BF16)

    def split(half, x, value):
        high = value.astype(BF16)
        packed[x, :, pl.ds(half * HALF, HALF)] = high
        packed[x, :, pl.ds(256 + half * HALF, HALF)] = (value - high.astype(F32)).astype(BF16)

    def x_copy(t, side):
        return pltpu.make_async_remote_copy(
            src_ref=send_x.at[t, 1 - side], dst_ref=halo_x.at[t, side],
            send_sem=xs_sem.at[t, side], recv_sem=xr_sem.at[t, side],
            device_id={"gx": gx + 1 if side == LO else gx - 1}, device_id_type=MESH)

    def y_copy(t, side):
        if side == LO:
            src = field.at[t, :, pl.ds(4, CX), pl.ds(20, 4), :]
            dst = halo_y_lo.at[t, :, :, pl.ds(4, 4), :]
        else:
            src = field.at[t, :, pl.ds(4, CX), pl.ds(8, 4), :]
            dst = halo_y_hi.at[t, :, :, pl.ds(8, 4), :]
        return pltpu.make_async_remote_copy(
            src_ref=src, dst_ref=dst, send_sem=ys_sem.at[t, side], recv_sem=yr_sem.at[t, side],
            device_id={"gy": gy + 1 if side == LO else gy - 1}, device_id_type=MESH)

    sends_x = {LO: gx < GX - 1, HI: gx > 0}
    gets_x = {LO: gx > 0, HI: gx < GX - 1}
    sends_y = {LO: gy < GY - 1, HI: gy > 0}
    gets_y = {LO: gy > 0, HI: gy < GY - 1}

    def each(conditions, make, t, act):
        for side in (LO, HI):
            @pl.when(conditions[side])
            def _():
                getattr(make(t, side), act)()

    EDGES = (0, 1, 2, 3, CX - 4, CX - 3, CX - 2, CX - 1)
    for half in range(2):
        for x in EDGES:
            pack_edge(0, half, x, field[0, half, 4 + x, pl.ds(8, CY), :])

    def split_plane(x, carry):
        for half in range(2):
            split(half, x, field[0, half, 4 + x, pl.ds(8, CY), :])
        return carry

    lax.fori_loop(0, CX, split_plane, 0)
    for i in (1, 2, 3, 5, 6, 7, 8):
        loads[i].wait()

    def base_step(t):
        def chunk(c, carry):
            x0 = pl.multiple_of(c * 8, 8)
            both = packed[pl.ds(x0, 8)].reshape(128, 512)
            along_z = jnp.dot(both, band_hi[...], preferred_element_type=F32)
            along_z += jnp.dot(both[:, :256], band_lo[...], preferred_element_type=F32)
            for half in range(2):
                planes = [field[t, half, x0 + j, pl.ds(8, CY), :] for j in range(16)]
                for i in range(8):
                    center = planes[i + 4]
                    lap = along_z[i * CY : (i + 1) * CY, half * HALF : (half + 1) * HALF] + (3.0 * COEFS[0]) * center
                    for k in range(1, 5):
                        lap += COEFS[k] * (
                            (planes[i + 4 - k] + planes[i + 4 + k])
                            + (field[t, half, x0 + 4 + i, pl.ds(8 - k, CY), :] + field[t, half, x0 + 4 + i, pl.ds(8 + k, CY), :]))
                    if t == 0:
                        before = prev[half, x0 + i]
                    else:
                        before = field[t - 1, half, x0 + 4 + i, pl.ds(8, CY), :] - source[t, half, x0 + i]
                    base[half, x0 + i] = 2.0 * center - before + c2[half, x0 + i] * lap
            return carry

        lax.fori_loop(0, CX // 8, chunk, 0)

    def fix_plane(t, half, x, across):
        low = high = None
        for k in range(1, 5):
            a = COEFS[k] * halo_y_lo[t, half, x, pl.ds(8 - k, 8), :]
            b = COEFS[k] * halo_y_hi[t, half, x, pl.ds(k, 8), :]
            low, high = (a, b) if low is None else (low + a, high + b)
        lap = jnp.concatenate([low, high], axis=0)
        if across is not None:
            lap += across
        value = base[half, x] + c2[half, x] * lap
        if t == 0:
            value += source[0, half, x]
        if t < STEPS - 1:
            field[t + 1, half, 4 + x, pl.ds(8, CY), :] = value
            split(half, x, value)
        if t == STEPS - 1:
            final[half, x] = value
        product = accel[t, half, x].astype(F32) * value
        fine[half, x] = product if t == 0 else fine[half, x] + product
        return value

    def fix_edges(t, side):
        for half in range(2):
            layer = [halo_x[t, side, half, j].astype(F32) for j in range(4)]
            near = 3 if side == LO else 0
            layer[near] += halo_x[t, side, half, 4].astype(F32)
            for j in range(4):
                x = j if side == LO else CX - 1 - j
                across = None
                for k in range(j + 1, 5):
                    away = k - j - 1
                    term = COEFS[k] * layer[3 - away if side == LO else away]
                    across = term if across is None else across + term
                value = fix_plane(t, half, x, across)
                if t < STEPS - 1:
                    pack_edge(t + 1, half, x, value)

    def fix_middle(t):
        def plane(x, carry):
            for half in range(2):
                fix_plane(t, half, x, None)
            return carry

        lax.fori_loop(4, CX - 4, plane, 0)

    def make_source(t):
        at, odd = t // 2, t % 2
        rows = traces[:, :, at, :].reshape(32, HALF)
        got = jnp.dot(pick[...].astype(BF16), rows.astype(BF16), preferred_element_type=F32)
        lane = iota((SLOTS, HALF), 1)
        keep = ((lane >> 6) == odd) & (((lane >> 4) & 3) == quarter)
        got = jnp.where(keep, got, 0.0).astype(BF16)
        wide = jnp.dot(got, spread[...], preferred_element_type=F32)
        own = (iota((SLOTS, 1024), 1) >> 4) == iota((SLOTS, 1024), 0)
        wide = jnp.where(own, wide, 0.0).astype(BF16)
        contribution = jnp.dot(wide, weights[...], preferred_element_type=F32)
        high = contribution.astype(BF16)
        low = (contribution - high.astype(F32)).astype(BF16)
        stacked = jnp.concatenate([high, low], axis=0)
        dense = jnp.dot(onehot[...], stacked, preferred_element_type=F32)
        for half in range(2):
            source[t, half] = dense[:, half * HALF : (half + 1) * HALF].reshape(CX, CY, HALF)

    base_step(0)

    pl.semaphore_wait(barrier, 31 + faces_half.astype(I32))

    def send_traces():
        return pltpu.make_async_remote_copy(
            src_ref=traces.at[spot, z_hi, pl.ds(0, 2)], dst_ref=traces.at[spot, z_hi, pl.ds(0, 2)],
            send_sem=zs_sem.at[0], recv_sem=zr_sem.at[0], device_id=partner, device_id_type=MESH)

    def get_traces():
        return pltpu.make_async_remote_copy(
            src_ref=traces.at[spot, 1 - z_hi, pl.ds(0, 2)], dst_ref=traces.at[spot, 1 - z_hi, pl.ds(0, 2)],
            send_sem=zs_sem.at[0], recv_sem=zr_sem.at[0], device_id=partner, device_id_type=MESH)

    def pass_traces(i):
        peer, _ = spot_peer(i)
        return pltpu.make_async_remote_copy(
            src_ref=traces.at[spot, :, pl.ds(0, 2)], dst_ref=traces.at[spot, :, pl.ds(0, 2)],
            send_sem=ts_sem.at[i], recv_sem=tr_sem.at[spot], device_id=peer, device_id_type=MESH)

    send_traces().start()
    each(sends_x, x_copy, 0, "start")
    each(sends_y, y_copy, 0, "start")
    get_traces().wait_recv()

    def start_trace(i, carry):
        pass_traces(i).start()
        return carry

    lax.fori_loop(1, 16, start_trace, 0)

    def wait_trace(i, carry):
        peer, other = spot_peer(i)
        pltpu.make_async_remote_copy(
            src_ref=traces.at[other, :, pl.ds(0, 2)], dst_ref=traces.at[other, :, pl.ds(0, 2)],
            send_sem=ts_sem.at[i], recv_sem=tr_sem.at[other], device_id=peer, device_id_type=MESH).wait_recv()
        return carry

    lax.fori_loop(1, 16, wait_trace, 0)
    make_source(0)

    pool = (flag((iota((256, 128), 0) >> 1) == iota((256, 128), 1)) * 0.125).astype(BF16)

    def restrict(first, rows):
        pairs = []
        for half in range(2):
            planes = fine[half, pl.ds(2 * first, 2 * rows)].reshape(rows, 2, CY, HALF)
            pairs.append((planes[:, 0] + planes[:, 1]).reshape(rows * CY, HALF))
        both = jnp.concatenate(pairs, axis=1)
        high = both.astype(BF16)
        left = both - high.astype(F32)
        mid = left.astype(BF16)
        last = (left - mid.astype(F32)).astype(BF16)
        pooled[pl.ds(0, rows * CY), :] = (
            jnp.dot(high, pool, preferred_element_type=F32)
            + jnp.dot(mid, pool, preferred_element_type=F32)
            + jnp.dot(last, pool, preferred_element_type=F32))
        size = rows * CY // 2
        coarse = pooled[pl.ds(0, size, stride=2), :] + pooled[pl.ds(1, size, stride=2), :]
        local[pl.ds(first, rows)] = coarse.reshape(rows, 8, HALF)

    EDGE_ROWS = (0, 1, CX // 2 - 2, CX // 2 - 1)
    owns = (shot >= 2) & (shot < SHOTS - 2)
    owns_edge = (shot >= 6) & (shot < 10)
    edge_row = jnp.where(shot < 8, shot - 6, shot + 6)

    def row_copy(r, source_shot):
        return pltpu.make_async_remote_copy(
            src_ref=local.at[r], dst_ref=arrived.at[source_shot],
            send_sem=rs_sem.at[r], recv_sem=rr_sem.at[source_shot], device_id={"shot": r}, device_id_type=MESH)

    def edge_copy(e, source_shot):
        return pltpu.make_async_remote_copy(
            src_ref=local.at[EDGE_ROWS[e]], dst_ref=arrived_edge.at[source_shot],
            send_sem=es_sem.at[e], recv_sem=er_sem.at[source_shot], device_id={"shot": 6 + e}, device_id_type=MESH)

    def sum_copy(i, r, sems):
        peer, _ = shot_peer(i)
        return pltpu.make_async_remote_copy(
            src_ref=total.at[r], dst_ref=total.at[r],
            send_sem=sems.at[i], recv_sem=ar_sem.at[r], device_id=peer, device_id_type=MESH)

    def rows_do(act):
        def one(r, carry):
            @pl.when(r != shot)
            def _():
                getattr(row_copy(r, shot), act)()
            return carry

        lax.fori_loop(2, SHOTS - 2, one, 0)

    def edges_do(act):
        for e in range(4):
            @pl.when(shot != 6 + e)
            def _():
                getattr(edge_copy(e, shot), act)()

    def sums_do(r, sems, act):
        def one(i, carry):
            getattr(sum_copy(i, r, sems), act)()
            return carry

        lax.fori_loop(1, SHOTS, one, 0)

    outs = []
    for half in range(2):
        lanes = pl.ds(half * HALF, HALF)
        outs.append(pltpu.make_async_copy(
            field.at[STEPS - 1, half, pl.ds(4, CX), pl.ds(8, CY), :], prev_o.at[:, :, lanes], out_sem.at[half]))
    for half in range(2):
        lanes = pl.ds(half * HALF, HALF)
        outs.append(pltpu.make_async_copy(final.at[half], cur_o.at[:, :, lanes], out_sem.at[2 + half]))

    for t in range(STEPS):
        last_step = t == STEPS - 1
        each(gets_y, y_copy, t, "wait_recv")
        if t > 0:
            fix_middle(t)
        if last_step:
            restrict(2, CX // 2 - 4)
            rows_do("start")
        each(gets_x, x_copy, t, "wait_recv")
        fix_edges(t, LO)
        fix_edges(t, HI)
        if not last_step:
            each(sends_x, x_copy, t + 1, "start")
        if t == 0:
            fix_middle(t)
        if t == STEPS - 2:
            for copy in outs[:2]:
                copy.start()
        if not last_step:
            each(sends_y, y_copy, t + 1, "start")
            make_source(t + 1)
            base_step(t + 1)

    restrict(0, 2)
    restrict(CX // 2 - 2, 2)
    edges_do("start")
    for copy in outs[2:]:
        copy.start()

    @pl.when(owns)
    def _():
        arrived[shot] = local[shot]

        def wait_row(i, carry):
            _, other = shot_peer(i)
            row_copy(shot, other).wait_recv()
            return carry

        lax.fori_loop(1, SHOTS, wait_row, 0)
        total[shot] = jnp.sum(arrived[...], axis=0)
        sums_do(shot, as_sem, "start")

    @pl.when(owns_edge)
    def _():
        arrived_edge[shot] = local[edge_row]

        def wait_edge(i, carry):
            _, other = shot_peer(i)
            edge_copy(0, other).wait_recv()
            return carry

        lax.fori_loop(1, SHOTS, wait_edge, 0)
        total[edge_row] = jnp.sum(arrived_edge[...], axis=0)
        sums_do(edge_row, bs_sem, "start")

    send_traces().wait_send()

    def end_trace(i, carry):
        pass_traces(i).wait_send()
        return carry

    lax.fori_loop(1, 16, end_trace, 0)
    for t in range(STEPS):
        each(sends_x, x_copy, t, "wait_send")
        each(sends_y, y_copy, t, "wait_send")
    rows_do("wait_send")
    edges_do("wait_send")

    def wait_sum(r, carry):
        @pl.when(r != shot)
        def _():
            sum_copy(1, r, as_sem).wait_recv()
        return carry

    lax.fori_loop(2, SHOTS - 2, wait_sum, 0)
    for e, r in enumerate(EDGE_ROWS):
        @pl.when(shot != 6 + e)
        def _():
            sum_copy(1, r, as_sem).wait_recv()

    last = pltpu.make_async_copy(total, grad_o, out_sem.at[4])
    last.start()
    for copy in outs:
        copy.wait()

    @pl.when(owns)
    def _():
        sums_do(shot, as_sem, "wait_send")

    @pl.when(owns_edge)
    def _():
        sums_do(edge_row, bs_sem, "wait_send")

    last.wait()


def hand_over(prev_i, cur_i, grad_i, prev_o, cur_o, grad_o, held, held_grad, in_sem, out_sem):
    steps = []
    for n in range(2 * PARTS):
        src, dst = ((prev_i, prev_o), (cur_i, cur_o))[n // PARTS]
        part = pl.ds(n % PARTS * (CX // PARTS), CX // PARTS)
        steps.append((
            pltpu.make_async_copy(src.at[part], held.at[n], in_sem.at[n]),
            pltpu.make_async_copy(held.at[n], dst.at[part], out_sem.at[n])))
    steps.append((
        pltpu.make_async_copy(grad_i, held_grad, in_sem.at[2 * PARTS]),
        pltpu.make_async_copy(held_grad, grad_o, out_sem.at[2 * PARTS])))
    for get, _ in steps:
        get.start()
    for get, put in steps:
        get.wait()
        put.start()
    for _, put in steps:
        put.wait()


def local_part(adj_prev, adj_cur, fwd_accel, courant2, traces, weights, rblock, column, counts):
    tile = (CX, CY, 2 * HALF)
    any_ = pl.BlockSpec(memory_space=pl.ANY)
    vmem = pl.BlockSpec(memory_space=pltpu.VMEM)
    dma = pltpu.SemaphoreType.DMA
    results = (
        jax.ShapeDtypeStruct(tile, F32),
        jax.ShapeDtypeStruct(tile, F32),
        jax.ShapeDtypeStruct((CX // 2, CY // 2, HALF), F32),
    )
    made = pl.pallas_call(
        kernel,
        out_shape=results,
        in_specs=[any_] * 8 + [pl.BlockSpec(memory_space=pltpu.HBM)],
        out_specs=(any_, any_, any_),
        scratch_shapes=[
            pltpu.VMEM((STEPS + 1, 2, CX + 8, 32, HALF), F32),
            pltpu.VMEM((2, CX, CY, HALF), F32),
            pltpu.VMEM((STEPS, 2, CX, CY, HALF), BF16),
            pltpu.VMEM((2, CX, CY, HALF), F32),
            pltpu.VMEM((SLOTS * RB, 256), BF16),
            pltpu.VMEM((1, STEPS, 64), BF16),
            pltpu.VMEM((1, SLOTS), I32),
            pltpu.VMEM((1, SLOTS), I32),
            pltpu.VMEM((1, 1), I32),
            pltpu.VMEM((2, CX, CY, HALF), F32),
            pltpu.VMEM((STEPS, 2, CX, CY, HALF), F32),
            pltpu.VMEM((2, CX, CY, HALF), F32),
            pltpu.VMEM((CX, CY, 512), BF16),
            pltpu.VMEM((512, 256), BF16),
            pltpu.VMEM((256, 256), BF16),
            pltpu.VMEM((STEPS, 2, CX, 16, HALF), F32),
            pltpu.VMEM((STEPS, 2, CX, 16, HALF), F32),
            pltpu.VMEM((STEPS, 2, 2, 5, CY, HALF), BF16),
            pltpu.VMEM((STEPS, 2, 2, 5, CY, HALF), BF16),
            pltpu.VMEM((16, 2, 8, HALF), F32),
            pltpu.VMEM((8, HALF), F32),
            pltpu.VMEM((128, 1024), BF16),
            pltpu.VMEM((CX * CY, 2 * SLOTS), BF16),
            pltpu.VMEM((SLOTS, 32), F32),
            pltpu.VMEM((192, HALF), F32),
            pltpu.VMEM((CX // 2, 8, HALF), F32),
            pltpu.VMEM((SHOTS, 8, HALF), F32),
            pltpu.VMEM((SHOTS, 8, HALF), F32),
            pltpu.VMEM((CX // 2, 8, HALF), F32),
            pltpu.VMEM((2, CX, CY, HALF), F32),
            dma((13,)),
            dma((STEPS, 2)), dma((STEPS, 2)), dma((STEPS, 2)), dma((STEPS, 2)),
            dma((1,)), dma((1,)), dma((16,)), dma((16,)),
            dma((SHOTS,)), dma((SHOTS,)), dma((4,)), dma((SHOTS,)), dma((SHOTS,)), dma((SHOTS,)), dma((SHOTS,)), dma((5,)),
        ],
        compiler_params=pltpu.CompilerParams(
            collective_id=0, has_side_effects=True, vmem_limit_bytes=56 << 20),
    )(
        adj_prev[0], adj_cur[0], fwd_accel[0], courant2, weights[0, 0].reshape(SLOTS * RB, 256),
        traces, rblock[0], column[0], counts,
    )
    previous, current, gradient = pl.pallas_call(
        hand_over,
        out_shape=results,
        in_specs=[any_] * 3,
        out_specs=(any_,) * 3,
        scratch_shapes=[
            pltpu.VMEM((2 * PARTS, CX // PARTS, CY, 2 * HALF), F32),
            pltpu.VMEM((CX // 2, CY // 2, HALF), F32),
            dma((2 * PARTS + 1,)), dma((2 * PARTS + 1,)),
        ],
        compiler_params=pltpu.CompilerParams(vmem_limit_bytes=56 << 20),
    )(*made)
    return previous[None], current[None], gradient


def solution(mesh):
    return jax.shard_map(
        local_part,
        mesh=mesh,
        in_specs=(
            P("shot", "gx", "gy", None),
            P("shot", "gx", "gy", None),
            P("shot", None, "gx", "gy", None),
            P("gx", "gy", None),
            P("shot", None, ("gx", "gy")),
            P("gx", "gy", None, None, None),
            P("gx", "gy", None),
            P("gx", "gy", None),
            P("gx", "gy"),
        ),
        out_specs=(P("shot", "gx", "gy", None), P("shot", "gx", "gy", None), P("gx", "gy", None)),
        check_vma=False,
    )
```

```python
import functools

import jax
import jax.numpy as jnp
import ml_dtypes
from jax import lax
from jax.experimental import pallas as pl
from jax.experimental.pallas import tpu as pltpu
from jax.sharding import PartitionSpec as P

MESH = pl.DeviceIdType.MESH
COEFS = (-205.0 / 72.0, 8.0 / 5.0, -1.0 / 5.0, 8.0 / 315.0, -1.0 / 560.0)
F32, BF16, I32 = jnp.float32, jnp.bfloat16, jnp.int32
STEPS, CX, CY, HALF = 4, 32, 16, 128
SLOTS, RB = 64, 16
GX, GY, SHOTS = 8, 4, 16
LO, HI = 0, 1
PARTS = 4


def iota(shape, dim):
    return lax.broadcasted_iota(I32, shape, dim)


def flag(condition):
    return jnp.where(condition, 1.0, 0.0).astype(F32)


def kernel(
    prev_h, cur_h, acc_h, c2_h, w_h, tr_h, rb_h, col_h, cnt_h,
    prev_o, cur_o, grad_o,
    field, prev, accel, c2, weights, tr_ref, rb_ref, col_ref, cnt_ref,
    base, source, fine, packed, band_hi, band_lo, halo_y_lo, halo_y_hi, halo_x, send_x,
    traces, block, spread, onehot, pick, pooled, local, arrived, from_twin, late_rows, total,
    in_sem, xs_sem, xr_sem, ys_sem, yr_sem, zs_sem, zr_sem, ts_sem, tr_sem, rs_sem, rr_sem, es_sem, er_sem, as_sem, ar_sem, bs_sem, br_sem,
):
    gx, gy, shot = lax.axis_index("gx"), lax.axis_index("gy"), lax.axis_index("shot")
    z_hi, row = lax.div(gx, 4), lax.rem(gx, 4)
    spot = row * 4 + gy

    def spot_peer(i):
        other = lax.rem(spot + i, 16)
        return {"gx": z_hi * 4 + lax.div(other, 4), "gy": lax.rem(other, 4)}, other

    partner = {"gx": lax.rem(gx + 4, GX)}
    faces_half = (gx == 3) | (gx == 4)

    def shot_peer(i):
        other = lax.rem(shot + i, SHOTS)
        return {"shot": other}, other

    barrier = pltpu.get_barrier_semaphore()

    def greet(device):
        pl.semaphore_signal(barrier, 1, device_id=device, device_id_type=MESH)

    greet(partner)

    @pl.when(faces_half)
    def _():
        greet({"gx": 7 - gx})

    def greet_shot(i, carry):
        greet(shot_peer(i)[0])
        return carry

    def greet_spot(i, carry):
        greet(spot_peer(i)[0])
        return carry

    lax.fori_loop(1, SHOTS, greet_shot, 0)
    lax.fori_loop(1, 16, greet_spot, 0)

    loads = []
    for half in range(2):
        lanes = pl.ds(half * HALF, HALF)
        loads.append(pltpu.make_async_copy(
            cur_h.at[:, :, lanes], field.at[0, half, pl.ds(4, CX), pl.ds(8, CY), :], in_sem.at[half]))
        loads.append(pltpu.make_async_copy(prev_h.at[:, :, lanes], prev.at[half], in_sem.at[2 + half]))
        loads.append(pltpu.make_async_copy(c2_h.at[:, :, lanes], c2.at[half], in_sem.at[4 + half]))
        loads.append(pltpu.make_async_copy(acc_h.at[:, :, :, lanes], accel.at[:, half], in_sem.at[6 + half]))
    loads.append(pltpu.make_async_copy(w_h, weights, in_sem.at[8]))
    for n, (src, dst) in enumerate(((tr_h, tr_ref), (rb_h, rb_ref), (col_h, col_ref), (cnt_h, cnt_ref))):
        loads.append(pltpu.make_async_copy(src, dst, in_sem.at[9 + n]))
    for copy in loads:
        copy.start()

    zero_rows = jnp.zeros((CX, 8, HALF), F32)
    zero_planes = jnp.zeros((4, 32, HALF), F32)
    for t in range(STEPS):
        for half in range(2):
            field[t, half, pl.ds(0, 4), :, :] = zero_planes
            field[t, half, pl.ds(4 + CX, 4), :, :] = zero_planes
            field[t, half, pl.ds(4, CX), pl.ds(0, 8), :] = zero_rows
            field[t, half, pl.ds(4, CX), pl.ds(24, 8), :] = zero_rows
            halo_y_lo[t, half, :, pl.ds(8, 8), :] = zero_rows
            halo_y_hi[t, half, :, pl.ds(0, 8), :] = zero_rows

    @pl.when(gx == 0)
    def _():
        halo_x[:, LO] = jnp.zeros((STEPS, 2, 5, CY, HALF), BF16)

    @pl.when(gx == GX - 1)
    def _():
        halo_x[:, HI] = jnp.zeros((STEPS, 2, 5, CY, HALF), BF16)

    @pl.when(gy == 0)
    def _():
        for t in range(STEPS):
            for half in range(2):
                halo_y_lo[t, half, :, pl.ds(0, 8), :] = zero_rows

    @pl.when(gy == GY - 1)
    def _():
        for t in range(STEPS):
            for half in range(2):
                halo_y_hi[t, half, :, pl.ds(8, 8), :] = zero_rows

    for copy in loads[9:]:
        copy.wait()

    block[...] = jnp.zeros((8, HALF), F32)
    block[pl.ds(0, STEPS), pl.ds(0, 64)] = tr_ref[0].astype(F32)
    as_is = block[...]
    turned = pltpu.roll(as_is, 64, 1)
    traces[spot, z_hi, pl.ds(0, 1), :] = as_is[0:1] + turned[1:2]
    traces[spot, z_hi, pl.ds(1, 1), :] = as_is[2:3] + turned[3:4]

    distance = jnp.abs(iota((256, 256), 0) - iota((256, 256), 1))
    band = jnp.zeros((256, 256), F32)
    rest = jnp.zeros((256, 256), F32)
    for k in range(1, 5):
        high = float(ml_dtypes.bfloat16(COEFS[k]))
        band = jnp.where(distance == k, high, band)
        rest = jnp.where(distance == k, COEFS[k] - high, rest)
    band_hi[pl.ds(0, 256), :] = band.astype(BF16)
    band_hi[pl.ds(256, 256), :] = band.astype(BF16)
    band_lo[...] = rest.astype(BF16)

    spread[...] = flag((iota((128, 1024), 0) & 15) == (iota((128, 1024), 1) & 15)).astype(BF16)
    slot_row = iota((1, SLOTS), 1)
    live = slot_row < cnt_ref[...]
    hit = flag((iota((CX * CY, SLOTS), 0) == col_ref[...]) & live).astype(BF16)
    onehot[...] = jnp.concatenate([hit, hit], axis=1)
    diagonal = iota((SLOTS, SLOTS), 0) == iota((SLOTS, SLOTS), 1)
    rb_column = jnp.sum(jnp.where(diagonal, rb_ref[...].astype(F32), 0.0), axis=1, keepdims=True).astype(I32)
    holder = rb_column >> 2
    pick[...] = flag(((holder & 15) * 2 + (holder >> 4)) == iota((SLOTS, 32), 1))
    quarter = rb_column & 3

    for copy in loads[0:8:4]:
        copy.wait()

    def pack_edge(t, half, x, value):
        high = value.astype(BF16)
        if x < 4:
            send_x[t, LO, half, x] = high
            if x == 0:
                send_x[t, LO, half, 4] = (value - high.astype(F32)).astype(BF16)
        if x >= CX - 4:
            send_x[t, HI, half, x - (CX - 4)] = high
            if x == CX - 1:
                send_x[t, HI, half, 4] = (value - high.astype(F32)).astype(BF16)

    def split(half, x, value):
        high = value.astype(BF16)
        packed[x, :, pl.ds(half * HALF, HALF)] = high
        packed[x, :, pl.ds(256 + half * HALF, HALF)] = (value - high.astype(F32)).astype(BF16)

    def x_copy(t, side):
        return pltpu.make_async_remote_copy(
            src_ref=send_x.at[t, 1 - side], dst_ref=halo_x.at[t, side],
            send_sem=xs_sem.at[t, side], recv_sem=xr_sem.at[t, side],
            device_id={"gx": gx + 1 if side == LO else gx - 1}, device_id_type=MESH)

    def y_copy(t, side):
        if side == LO:
            src = field.at[t, :, pl.ds(4, CX), pl.ds(20, 4), :]
            dst = halo_y_lo.at[t, :, :, pl.ds(4, 4), :]
        else:
            src = field.at[t, :, pl.ds(4, CX), pl.ds(8, 4), :]
            dst = halo_y_hi.at[t, :, :, pl.ds(8, 4), :]
        return pltpu.make_async_remote_copy(
            src_ref=src, dst_ref=dst, send_sem=ys_sem.at[t, side], recv_sem=yr_sem.at[t, side],
            device_id={"gy": gy + 1 if side == LO else gy - 1}, device_id_type=MESH)

    sends_x = {LO: gx < GX - 1, HI: gx > 0}
    gets_x = {LO: gx > 0, HI: gx < GX - 1}
    sends_y = {LO: gy < GY - 1, HI: gy > 0}
    gets_y = {LO: gy > 0, HI: gy < GY - 1}

    def each(conditions, make, t, act):
        for side in (LO, HI):
            @pl.when(conditions[side])
            def _():
                getattr(make(t, side), act)()

    EDGES = (0, 1, 2, 3, CX - 4, CX - 3, CX - 2, CX - 1)
    for half in range(2):
        for x in EDGES:
            pack_edge(0, half, x, field[0, half, 4 + x, pl.ds(8, CY), :])

    def split_plane(x, carry):
        for half in range(2):
            split(half, x, field[0, half, 4 + x, pl.ds(8, CY), :])
        return carry

    lax.fori_loop(0, CX, split_plane, 0)
    for i in (1, 2, 3, 5, 6, 7, 8):
        loads[i].wait()

    def base_step(t):
        def chunk(c, carry):
            x0 = pl.multiple_of(c * 8, 8)
            both = packed[pl.ds(x0, 8)].reshape(128, 512)
            along_z = jnp.dot(both, band_hi[...], preferred_element_type=F32)
            along_z += jnp.dot(both[:, :256], band_lo[...], preferred_element_type=F32)
            for half in range(2):
                planes = [field[t, half, x0 + j, pl.ds(8, CY), :] for j in range(16)]
                for i in range(8):
                    center = planes[i + 4]
                    lap = along_z[i * CY : (i + 1) * CY, half * HALF : (half + 1) * HALF] + (3.0 * COEFS[0]) * center
                    for k in range(1, 5):
                        lap += COEFS[k] * (
                            (planes[i + 4 - k] + planes[i + 4 + k])
                            + (field[t, half, x0 + 4 + i, pl.ds(8 - k, CY), :] + field[t, half, x0 + 4 + i, pl.ds(8 + k, CY), :]))
                    if t == 0:
                        before = prev[half, x0 + i]
                    else:
                        before = field[t - 1, half, x0 + 4 + i, pl.ds(8, CY), :] - source[t, half, x0 + i]
                    base[half, x0 + i] = 2.0 * center - before + c2[half, x0 + i] * lap
            return carry

        lax.fori_loop(0, CX // 8, chunk, 0)

    def fix_plane(t, half, x, across):
        low = high = None
        for k in range(1, 5):
            a = COEFS[k] * halo_y_lo[t, half, x, pl.ds(8 - k, 8), :]
            b = COEFS[k] * halo_y_hi[t, half, x, pl.ds(k, 8), :]
            low, high = (a, b) if low is None else (low + a, high + b)
        lap = jnp.concatenate([low, high], axis=0)
        if across is not None:
            lap += across
        value = base[half, x] + c2[half, x] * lap
        if t == 0:
            value += source[0, half, x]
        if t < STEPS - 1:
            field[t + 1, half, 4 + x, pl.ds(8, CY), :] = value
            split(half, x, value)
        if t >= STEPS - 2:
            (prev_o if t == STEPS - 2 else cur_o)[x, :, pl.ds(half * HALF, HALF)] = value
        product = accel[t, half, x].astype(F32) * value
        fine[half, x] = product if t == 0 else fine[half, x] + product
        return value

    def fix_edges(t, side):
        for half in range(2):
            layer = [halo_x[t, side, half, j].astype(F32) for j in range(4)]
            near = 3 if side == LO else 0
            layer[near] += halo_x[t, side, half, 4].astype(F32)
            for j in range(4):
                x = j if side == LO else CX - 1 - j
                across = None
                for k in range(j + 1, 5):
                    away = k - j - 1
                    term = COEFS[k] * layer[3 - away if side == LO else away]
                    across = term if across is None else across + term
                value = fix_plane(t, half, x, across)
                if t < STEPS - 1:
                    pack_edge(t + 1, half, x, value)

    def fix_middle(t):
        def plane(x, carry):
            for half in range(2):
                fix_plane(t, half, x, None)
            return carry

        lax.fori_loop(4, CX - 4, plane, 0)

    def make_source(t):
        at, odd = t // 2, t % 2
        rows = traces[:, :, at, :].reshape(32, HALF)
        got = jnp.dot(pick[...].astype(BF16), rows.astype(BF16), preferred_element_type=F32)
        lane = iota((SLOTS, HALF), 1)
        keep = ((lane >> 6) == odd) & (((lane >> 4) & 3) == quarter)
        got = jnp.where(keep, got, 0.0).astype(BF16)
        wide = jnp.dot(got, spread[...], preferred_element_type=F32)
        own = (iota((SLOTS, 1024), 1) >> 4) == iota((SLOTS, 1024), 0)
        wide = jnp.where(own, wide, 0.0).astype(BF16)
        contribution = jnp.dot(wide, weights[...], preferred_element_type=F32)
        high = contribution.astype(BF16)
        low = (contribution - high.astype(F32)).astype(BF16)
        stacked = jnp.concatenate([high, low], axis=0)
        dense = jnp.dot(onehot[...], stacked, preferred_element_type=F32)
        for half in range(2):
            source[t, half] = dense[:, half * HALF : (half + 1) * HALF].reshape(CX, CY, HALF)

    base_step(0)

    pl.semaphore_wait(barrier, 31 + faces_half.astype(I32))

    def send_traces():
        return pltpu.make_async_remote_copy(
            src_ref=traces.at[spot, z_hi, pl.ds(0, 2)], dst_ref=traces.at[spot, z_hi, pl.ds(0, 2)],
            send_sem=zs_sem.at[0], recv_sem=zr_sem.at[0], device_id=partner, device_id_type=MESH)

    def get_traces():
        return pltpu.make_async_remote_copy(
            src_ref=traces.at[spot, 1 - z_hi, pl.ds(0, 2)], dst_ref=traces.at[spot, 1 - z_hi, pl.ds(0, 2)],
            send_sem=zs_sem.at[0], recv_sem=zr_sem.at[0], device_id=partner, device_id_type=MESH)

    def pass_traces(i):
        peer, _ = spot_peer(i)
        return pltpu.make_async_remote_copy(
            src_ref=traces.at[spot, :, pl.ds(0, 2)], dst_ref=traces.at[spot, :, pl.ds(0, 2)],
            send_sem=ts_sem.at[i], recv_sem=tr_sem.at[spot], device_id=peer, device_id_type=MESH)

    send_traces().start()
    each(sends_x, x_copy, 0, "start")
    each(sends_y, y_copy, 0, "start")
    get_traces().wait_recv()

    def start_trace(i, carry):
        pass_traces(i).start()
        return carry

    lax.fori_loop(1, 16, start_trace, 0)

    def wait_trace(i, carry):
        peer, other = spot_peer(i)
        pltpu.make_async_remote_copy(
            src_ref=traces.at[other, :, pl.ds(0, 2)], dst_ref=traces.at[other, :, pl.ds(0, 2)],
            send_sem=ts_sem.at[i], recv_sem=tr_sem.at[other], device_id=peer, device_id_type=MESH).wait_recv()
        return carry

    lax.fori_loop(1, 16, wait_trace, 0)
    make_source(0)

    pool = (flag((iota((256, 128), 0) >> 1) == iota((256, 128), 1)) * 0.125).astype(BF16)

    def restrict(first, rows):
        pairs = []
        for half in range(2):
            planes = fine[half, pl.ds(2 * first, 2 * rows)].reshape(rows, 2, CY, HALF)
            pairs.append((planes[:, 0] + planes[:, 1]).reshape(rows * CY, HALF))
        both = jnp.concatenate(pairs, axis=1)
        high = both.astype(BF16)
        left = both - high.astype(F32)
        mid = left.astype(BF16)
        last = (left - mid.astype(F32)).astype(BF16)
        pooled[pl.ds(0, rows * CY), :] = (
            jnp.dot(high, pool, preferred_element_type=F32)
            + jnp.dot(mid, pool, preferred_element_type=F32)
            + jnp.dot(last, pool, preferred_element_type=F32))
        size = rows * CY // 2
        coarse = pooled[pl.ds(0, size, stride=2), :] + pooled[pl.ds(1, size, stride=2), :]
        local[pl.ds(first, rows)] = coarse.reshape(rows, 8, HALF)

    late = jnp.where(gx < GX // 2, CX // 2 - 2, 0)
    early = jnp.where(gx < GX // 2, 0, 2)
    OWNERS = range(4, 11)
    owns = (shot >= OWNERS[0]) & (shot <= OWNERS[-1])
    core = lax.rem(shot, 2)
    twin = {"shot": shot + 1 - 2 * core}

    def pair_of(owner):
        return pl.ds(early + 2 * (owner - OWNERS[0]), 2)

    def row_copy(owner, source_shot):
        return pltpu.make_async_remote_copy(
            src_ref=local.at[pair_of(owner)], dst_ref=arrived.at[source_shot],
            send_sem=rs_sem.at[owner], recv_sem=rr_sem.at[source_shot], device_id={"shot": owner}, device_id_type=MESH)

    def sum_copy(i, owner):
        peer, _ = shot_peer(i)
        return pltpu.make_async_remote_copy(
            src_ref=total.at[pair_of(owner)], dst_ref=total.at[pair_of(owner)],
            send_sem=as_sem.at[i], recv_sem=ar_sem.at[owner], device_id=peer, device_id_type=MESH)

    def twin_copy():
        return pltpu.make_async_remote_copy(
            src_ref=local.at[late + 1 - core], dst_ref=from_twin,
            send_sem=es_sem.at[0], recv_sem=er_sem.at[0], device_id=twin, device_id_type=MESH)

    def late_copy(i, source_shot):
        peer, _ = shot_peer(i)
        return pltpu.make_async_remote_copy(
            src_ref=late_rows.at[source_shot], dst_ref=late_rows.at[source_shot],
            send_sem=bs_sem.at[i], recv_sem=br_sem.at[source_shot], device_id=peer, device_id_type=MESH)

    def rows_do(act):
        for owner in OWNERS:
            @pl.when(owner != shot)
            def _():
                getattr(row_copy(owner, shot), act)()

    def shots_do(make, act):
        def one(i, carry):
            getattr(make(i), act)()
            return carry

        lax.fori_loop(1, SHOTS, one, 0)

    for t in range(STEPS - 1):
        each(gets_y, y_copy, t, "wait_recv")
        if t > 0:
            fix_middle(t)
        each(gets_x, x_copy, t, "wait_recv")
        fix_edges(t, LO)
        fix_edges(t, HI)
        each(sends_x, x_copy, t + 1, "start")
        if t == 0:
            fix_middle(t)
        each(sends_y, y_copy, t + 1, "start")
        make_source(t + 1)
        base_step(t + 1)

    t = STEPS - 1
    each(gets_y, y_copy, t, "wait_recv")
    fix_middle(t)

    def edge(side):
        @pl.when(gets_x[side])
        def _():
            x_copy(t, side).wait_recv()

        fix_edges(t, side)

    lower = gx < GX // 2

    @pl.when(lower)
    def _():
        edge(LO)
        restrict(0, CX // 2 - 2)

    @pl.when(jnp.logical_not(lower))
    def _():
        edge(HI)
        restrict(2, CX // 2 - 2)

    rows_do("start")

    @pl.when(lower)
    def _():
        edge(HI)
        restrict(CX // 2 - 2, 2)

    @pl.when(jnp.logical_not(lower))
    def _():
        edge(LO)
        restrict(0, 2)

    twin_copy().start()
    twin_copy().wait_recv()
    late_rows[shot] = local[late + core] + from_twin[...]
    shots_do(lambda i: late_copy(i, shot), "start")

    @pl.when(owns)
    def _():
        arrived[shot] = local[pair_of(shot)]
        shots_do(lambda i: row_copy(shot, shot_peer(i)[1]), "wait_recv")
        total[pair_of(shot)] = jnp.sum(arrived[...], axis=0)
        shots_do(lambda i: sum_copy(i, shot), "start")

    send_traces().wait_send()

    def end_trace(i, carry):
        pass_traces(i).wait_send()
        return carry

    lax.fori_loop(1, 16, end_trace, 0)
    for t in range(STEPS):
        each(sends_x, x_copy, t, "wait_send")
        each(sends_y, y_copy, t, "wait_send")
    rows_do("wait_send")
    twin_copy().wait_send()
    for owner in OWNERS:
        @pl.when(owner != shot)
        def _():
            sum_copy(1, owner).wait_recv()
    shots_do(lambda i: late_copy(i, shot_peer(i)[1]), "wait_recv")
    every = late_rows[...].reshape(SHOTS // 2, 2, 8, HALF)
    total[pl.ds(late, 2)] = jnp.sum(every, axis=0)

    grad_o[...] = total[...]

    shots_do(lambda i: late_copy(i, shot), "wait_send")

    @pl.when(owns)
    def _():
        shots_do(lambda i: sum_copy(i, shot), "wait_send")


def hand_over(prev_i, cur_i, grad_i, prev_o, cur_o, grad_o, sem):
    copies = []
    for n in range(2 * PARTS):
        src, dst = ((prev_i, prev_o), (cur_i, cur_o))[n // PARTS]
        part = pl.ds(n % PARTS * (CX // PARTS), CX // PARTS)
        copies.append(pltpu.make_async_copy(src.at[part], dst.at[part], sem.at[n]))
    copies.append(pltpu.make_async_copy(grad_i, grad_o, sem.at[2 * PARTS]))
    for copy in copies:
        copy.start()
    for copy in copies:
        copy.wait()


def local_part(adj_prev, adj_cur, fwd_accel, courant2, traces, weights, rblock, column, counts):
    tile = (CX, CY, 2 * HALF)
    any_ = pl.BlockSpec(memory_space=pl.ANY)
    vmem = pl.BlockSpec(memory_space=pltpu.VMEM)
    dma = pltpu.SemaphoreType.DMA
    results = (
        jax.ShapeDtypeStruct(tile, F32),
        jax.ShapeDtypeStruct(tile, F32),
        jax.ShapeDtypeStruct((CX // 2, CY // 2, HALF), F32),
    )
    made = pl.pallas_call(
        kernel,
        out_shape=results,
        in_specs=[any_] * 9,
        out_specs=(vmem, vmem, vmem),
        scratch_shapes=[
            pltpu.VMEM((STEPS + 1, 2, CX + 8, 32, HALF), F32),
            pltpu.VMEM((2, CX, CY, HALF), F32),
            pltpu.VMEM((STEPS, 2, CX, CY, HALF), BF16),
            pltpu.VMEM((2, CX, CY, HALF), F32),
            pltpu.VMEM((SLOTS * RB, 256), BF16),
            pltpu.VMEM((1, STEPS, 64), BF16),
            pltpu.VMEM((1, SLOTS), I32),
            pltpu.VMEM((1, SLOTS), I32),
            pltpu.VMEM((1, 1), I32),
            pltpu.VMEM((2, CX, CY, HALF), F32),
            pltpu.VMEM((STEPS, 2, CX, CY, HALF), F32),
            pltpu.VMEM((2, CX, CY, HALF), F32),
            pltpu.VMEM((CX, CY, 512), BF16),
            pltpu.VMEM((512, 256), BF16),
            pltpu.VMEM((256, 256), BF16),
            pltpu.VMEM((STEPS, 2, CX, 16, HALF), F32),
            pltpu.VMEM((STEPS, 2, CX, 16, HALF), F32),
            pltpu.VMEM((STEPS, 2, 2, 5, CY, HALF), BF16),
            pltpu.VMEM((STEPS, 2, 2, 5, CY, HALF), BF16),
            pltpu.VMEM((16, 2, 8, HALF), F32),
            pltpu.VMEM((8, HALF), F32),
            pltpu.VMEM((128, 1024), BF16),
            pltpu.VMEM((CX * CY, 2 * SLOTS), BF16),
            pltpu.VMEM((SLOTS, 32), F32),
            pltpu.VMEM((224, HALF), F32),
            pltpu.VMEM((CX // 2, 8, HALF), F32),
            pltpu.VMEM((SHOTS, 2, 8, HALF), F32),
            pltpu.VMEM((8, HALF), F32),
            pltpu.VMEM((SHOTS, 8, HALF), F32),
            pltpu.VMEM((CX // 2, 8, HALF), F32),
            dma((13,)),
            dma((STEPS, 2)), dma((STEPS, 2)), dma((STEPS, 2)), dma((STEPS, 2)),
            dma((1,)), dma((1,)), dma((16,)), dma((16,)),
            dma((SHOTS,)), dma((SHOTS,)), dma((1,)), dma((1,)), dma((SHOTS,)), dma((SHOTS,)), dma((SHOTS,)), dma((SHOTS,)),
        ],
        compiler_params=pltpu.CompilerParams(
            collective_id=0, has_side_effects=True, vmem_limit_bytes=53760 << 10),
    )(
        adj_prev[0], adj_cur[0], fwd_accel[0], courant2, weights[0, 0].reshape(SLOTS * RB, 256),
        traces, rblock[0], column[0], counts,
    )
    previous, current, gradient = pl.pallas_call(
        hand_over,
        out_shape=results,
        in_specs=[vmem] * 3,
        out_specs=(any_,) * 3,
        scratch_shapes=[dma((2 * PARTS + 1,))],
        compiler_params=pltpu.CompilerParams(vmem_limit_bytes=16 << 20),
    )(*made)
    return previous[None], current[None], gradient


def solution(mesh):
    return jax.shard_map(
        local_part,
        mesh=mesh,
        in_specs=(
            P("shot", "gx", "gy", None),
            P("shot", "gx", "gy", None),
            P("shot", None, "gx", "gy", None),
            P("gx", "gy", None),
            P("shot", None, ("gx", "gy")),
            P("gx", "gy", None, None, None),
            P("gx", "gy", None),
            P("gx", "gy", None),
            P("gx", "gy"),
        ),
        out_specs=(P("shot", "gx", "gy", None), P("shot", "gx", "gy", None), P("gx", "gy", None)),
        check_vma=False,
    )
```

```python
import functools

import jax
import jax.numpy as jnp
import ml_dtypes
from jax import lax
from jax.experimental import pallas as pl
from jax.experimental.pallas import tpu as pltpu
from jax.sharding import PartitionSpec as P

MESH = pl.DeviceIdType.MESH
COEFS = (-205.0 / 72.0, 8.0 / 5.0, -1.0 / 5.0, 8.0 / 315.0, -1.0 / 560.0)
F32, BF16, I32 = jnp.float32, jnp.bfloat16, jnp.int32
STEPS, CX, CY, HALF = 4, 32, 16, 128
SLOTS, RB = 64, 16
GX, GY, SHOTS = 8, 4, 16
LO, HI = 0, 1
PARTS = 4


def iota(shape, dim):
    return lax.broadcasted_iota(I32, shape, dim)


def flag(condition):
    return jnp.where(condition, 1.0, 0.0).astype(F32)


def kernel(
    prev_h, cur_h, acc_h, c2_h, w_h, tr_h, rb_h, col_h, cnt_h,
    prev_o, cur_o, grad_o,
    field, prev, accel, c2, weights, tr_ref, rb_ref, col_ref, cnt_ref,
    base, source, fine, packed, band_hi, band_lo, halo_y_lo, halo_y_hi, halo_x, send_x,
    traces, block, spread, onehot, pick, pooled, local, arrived, from_twin, late_rows, total,
    in_sem, xs_sem, xr_sem, ys_sem, yr_sem, zs_sem, zr_sem, ts_sem, tr_sem, rs_sem, rr_sem, es_sem, er_sem, as_sem, ar_sem, bs_sem, br_sem,
):
    gx, gy, shot = lax.axis_index("gx"), lax.axis_index("gy"), lax.axis_index("shot")
    z_hi, row = lax.div(gx, 4), lax.rem(gx, 4)
    spot = row * 4 + gy

    def spot_peer(i):
        other = lax.rem(spot + i, 16)
        return {"gx": z_hi * 4 + lax.div(other, 4), "gy": lax.rem(other, 4)}, other

    partner = {"gx": lax.rem(gx + 4, GX)}
    faces_half = (gx == 3) | (gx == 4)

    def shot_peer(i):
        other = lax.rem(shot + i, SHOTS)
        return {"shot": other}, other

    barrier = pltpu.get_barrier_semaphore()

    def greet(device):
        pl.semaphore_signal(barrier, 1, device_id=device, device_id_type=MESH)

    greet(partner)

    @pl.when(faces_half)
    def _():
        greet({"gx": 7 - gx})

    def greet_shot(i, carry):
        greet(shot_peer(i)[0])
        return carry

    def greet_spot(i, carry):
        greet(spot_peer(i)[0])
        return carry

    lax.fori_loop(1, SHOTS, greet_shot, 0)
    lax.fori_loop(1, 16, greet_spot, 0)

    loads = []
    for half in range(2):
        lanes = pl.ds(half * HALF, HALF)
        loads.append(pltpu.make_async_copy(
            cur_h.at[:, :, lanes], field.at[0, half, pl.ds(4, CX), pl.ds(8, CY), :], in_sem.at[half]))
        loads.append(pltpu.make_async_copy(prev_h.at[:, :, lanes], prev.at[half], in_sem.at[2 + half]))
        loads.append(pltpu.make_async_copy(c2_h.at[:, :, lanes], c2.at[half], in_sem.at[4 + half]))
        loads.append(pltpu.make_async_copy(acc_h.at[:, :, :, lanes], accel.at[:, half], in_sem.at[6 + half]))
    loads.append(pltpu.make_async_copy(w_h, weights, in_sem.at[8]))
    for n, (src, dst) in enumerate(((tr_h, tr_ref), (rb_h, rb_ref), (col_h, col_ref), (cnt_h, cnt_ref))):
        loads.append(pltpu.make_async_copy(src, dst, in_sem.at[9 + n]))
    for copy in loads:
        copy.start()

    zero_rows = jnp.zeros((CX, 8, HALF), F32)
    zero_planes = jnp.zeros((4, 32, HALF), F32)
    for t in range(STEPS):
        for half in range(2):
            field[t, half, pl.ds(0, 4), :, :] = zero_planes
            field[t, half, pl.ds(4 + CX, 4), :, :] = zero_planes
            field[t, half, pl.ds(4, CX), pl.ds(0, 8), :] = zero_rows
            field[t, half, pl.ds(4, CX), pl.ds(24, 8), :] = zero_rows
            halo_y_lo[t, half, :, pl.ds(8, 8), :] = zero_rows
            halo_y_hi[t, half, :, pl.ds(0, 8), :] = zero_rows

    @pl.when(gx == 0)
    def _():
        halo_x[:, LO] = jnp.zeros((STEPS, 2, 5, CY, HALF), BF16)

    @pl.when(gx == GX - 1)
    def _():
        halo_x[:, HI] = jnp.zeros((STEPS, 2, 5, CY, HALF), BF16)

    @pl.when(gy == 0)
    def _():
        for t in range(STEPS):
            for half in range(2):
                halo_y_lo[t, half, :, pl.ds(0, 8), :] = zero_rows

    @pl.when(gy == GY - 1)
    def _():
        for t in range(STEPS):
            for half in range(2):
                halo_y_hi[t, half, :, pl.ds(8, 8), :] = zero_rows

    for copy in loads[9:]:
        copy.wait()

    block[...] = jnp.zeros((8, HALF), F32)
    block[pl.ds(0, STEPS), pl.ds(0, 64)] = tr_ref[0].astype(F32)
    as_is = block[...]
    turned = pltpu.roll(as_is, 64, 1)
    traces[spot, z_hi, pl.ds(0, 1), :] = as_is[0:1] + turned[1:2]
    traces[spot, z_hi, pl.ds(1, 1), :] = as_is[2:3] + turned[3:4]

    distance = jnp.abs(iota((256, 256), 0) - iota((256, 256), 1))
    band = jnp.zeros((256, 256), F32)
    rest = jnp.zeros((256, 256), F32)
    for k in range(1, 5):
        high = float(ml_dtypes.bfloat16(COEFS[k]))
        band = jnp.where(distance == k, high, band)
        rest = jnp.where(distance == k, COEFS[k] - high, rest)
    band_hi[pl.ds(0, 256), :] = band.astype(BF16)
    band_hi[pl.ds(256, 256), :] = band.astype(BF16)
    band_lo[...] = rest.astype(BF16)

    spread[...] = flag((iota((128, 1024), 0) & 15) == (iota((128, 1024), 1) & 15)).astype(BF16)
    slot_row = iota((1, SLOTS), 1)
    live = slot_row < cnt_ref[...]
    hit = flag((iota((CX * CY, SLOTS), 0) == col_ref[...]) & live).astype(BF16)
    onehot[...] = jnp.concatenate([hit, hit], axis=1)
    diagonal = iota((SLOTS, SLOTS), 0) == iota((SLOTS, SLOTS), 1)
    rb_column = jnp.sum(jnp.where(diagonal, rb_ref[...].astype(F32), 0.0), axis=1, keepdims=True).astype(I32)
    holder = rb_column >> 2
    pick[...] = flag(((holder & 15) * 2 + (holder >> 4)) == iota((SLOTS, 32), 1))
    quarter = rb_column & 3

    for copy in loads[0:8:4]:
        copy.wait()

    def pack_edge(t, half, x, value):
        high = value.astype(BF16)
        if x < 4:
            send_x[t, LO, half, x] = high
            if x == 0:
                send_x[t, LO, half, 4] = (value - high.astype(F32)).astype(BF16)
        if x >= CX - 4:
            send_x[t, HI, half, x - (CX - 4)] = high
            if x == CX - 1:
                send_x[t, HI, half, 4] = (value - high.astype(F32)).astype(BF16)

    def split(half, x, value):
        high = value.astype(BF16)
        packed[x, :, pl.ds(half * HALF, HALF)] = high
        packed[x, :, pl.ds(256 + half * HALF, HALF)] = (value - high.astype(F32)).astype(BF16)

    def x_copy(t, side):
        return pltpu.make_async_remote_copy(
            src_ref=send_x.at[t, 1 - side], dst_ref=halo_x.at[t, side],
            send_sem=xs_sem.at[t, side], recv_sem=xr_sem.at[t, side],
            device_id={"gx": gx + 1 if side == LO else gx - 1}, device_id_type=MESH)

    PIECES = ((4, CX - 8), (0, 4), (CX - 4, 4))

    def y_copy(t, side, piece):
        first, planes = PIECES[piece]
        inner = pl.ds(4 + first, planes)
        outer = pl.ds(first, planes)
        if side == LO:
            src = field.at[t, :, inner, pl.ds(20, 4), :]
            dst = halo_y_lo.at[t, :, outer, pl.ds(4, 4), :]
        else:
            src = field.at[t, :, inner, pl.ds(8, 4), :]
            dst = halo_y_hi.at[t, :, outer, pl.ds(8, 4), :]
        return pltpu.make_async_remote_copy(
            src_ref=src, dst_ref=dst, send_sem=ys_sem.at[t, side, piece], recv_sem=yr_sem.at[t, side, piece],
            device_id={"gy": gy + 1 if side == LO else gy - 1}, device_id_type=MESH)

    sends_x = {LO: gx < GX - 1, HI: gx > 0}
    gets_x = {LO: gx > 0, HI: gx < GX - 1}
    sends_y = {LO: gy < GY - 1, HI: gy > 0}
    gets_y = {LO: gy > 0, HI: gy < GY - 1}

    def each(conditions, make, t, act):
        for side in (LO, HI):
            @pl.when(conditions[side])
            def _():
                getattr(make(t, side), act)()

    def each_y(conditions, pieces, t, act):
        for piece in pieces:
            each(conditions, lambda step, side, piece=piece: y_copy(step, side, piece), t, act)

    MIDDLE, OUTER, ALL = (0,), (1, 2), (0, 1, 2)

    EDGES = (0, 1, 2, 3, CX - 4, CX - 3, CX - 2, CX - 1)
    for half in range(2):
        for x in EDGES:
            pack_edge(0, half, x, field[0, half, 4 + x, pl.ds(8, CY), :])

    def split_plane(x, carry):
        for half in range(2):
            split(half, x, field[0, half, 4 + x, pl.ds(8, CY), :])
        return carry

    lax.fori_loop(0, CX, split_plane, 0)
    for i in (1, 2, 3, 5, 6, 7, 8):
        loads[i].wait()

    def base_step(t):
        def chunk(c, carry):
            x0 = pl.multiple_of(c * 8, 8)
            both = packed[pl.ds(x0, 8)].reshape(128, 512)
            along_z = jnp.dot(both, band_hi[...], preferred_element_type=F32)
            along_z += jnp.dot(both[:, :256], band_lo[...], preferred_element_type=F32)
            for half in range(2):
                planes = [field[t, half, x0 + j, pl.ds(8, CY), :] for j in range(16)]
                for i in range(8):
                    center = planes[i + 4]
                    lap = along_z[i * CY : (i + 1) * CY, half * HALF : (half + 1) * HALF] + (3.0 * COEFS[0]) * center
                    for k in range(1, 5):
                        lap += COEFS[k] * (
                            (planes[i + 4 - k] + planes[i + 4 + k])
                            + (field[t, half, x0 + 4 + i, pl.ds(8 - k, CY), :] + field[t, half, x0 + 4 + i, pl.ds(8 + k, CY), :]))
                    if t == 0:
                        before = prev[half, x0 + i]
                    else:
                        before = field[t - 1, half, x0 + 4 + i, pl.ds(8, CY), :] - source[t, half, x0 + i]
                    base[half, x0 + i] = 2.0 * center - before + c2[half, x0 + i] * lap
            return carry

        lax.fori_loop(0, CX // 8, chunk, 0)

    def fix_plane(t, half, x, across):
        low = high = None
        for k in range(1, 5):
            a = COEFS[k] * halo_y_lo[t, half, x, pl.ds(8 - k, 8), :]
            b = COEFS[k] * halo_y_hi[t, half, x, pl.ds(k, 8), :]
            low, high = (a, b) if low is None else (low + a, high + b)
        lap = jnp.concatenate([low, high], axis=0)
        if across is not None:
            lap += across
        value = base[half, x] + c2[half, x] * lap
        if t == 0:
            value += source[0, half, x]
        if t < STEPS - 1:
            field[t + 1, half, 4 + x, pl.ds(8, CY), :] = value
            split(half, x, value)
        if t >= STEPS - 2:
            (prev_o if t == STEPS - 2 else cur_o)[x, :, pl.ds(half * HALF, HALF)] = value
        product = accel[t, half, x].astype(F32) * value
        fine[half, x] = product if t == 0 else fine[half, x] + product
        return value

    def fix_edges(t, side):
        for half in range(2):
            layer = [halo_x[t, side, half, j].astype(F32) for j in range(4)]
            near = 3 if side == LO else 0
            layer[near] += halo_x[t, side, half, 4].astype(F32)
            for j in range(4):
                x = j if side == LO else CX - 1 - j
                across = None
                for k in range(j + 1, 5):
                    away = k - j - 1
                    term = COEFS[k] * layer[3 - away if side == LO else away]
                    across = term if across is None else across + term
                value = fix_plane(t, half, x, across)
                if t < STEPS - 1:
                    pack_edge(t + 1, half, x, value)

    def fix_middle(t):
        def plane(x, carry):
            for half in range(2):
                fix_plane(t, half, x, None)
            return carry

        lax.fori_loop(4, CX - 4, plane, 0)

    def make_source(t):
        at, odd = t // 2, t % 2
        rows = traces[:, :, at, :].reshape(32, HALF)
        got = jnp.dot(pick[...].astype(BF16), rows.astype(BF16), preferred_element_type=F32)
        lane = iota((SLOTS, HALF), 1)
        keep = ((lane >> 6) == odd) & (((lane >> 4) & 3) == quarter)
        got = jnp.where(keep, got, 0.0).astype(BF16)
        wide = jnp.dot(got, spread[...], preferred_element_type=F32)
        own = (iota((SLOTS, 1024), 1) >> 4) == iota((SLOTS, 1024), 0)
        wide = jnp.where(own, wide, 0.0).astype(BF16)
        contribution = jnp.dot(wide, weights[...], preferred_element_type=F32)
        high = contribution.astype(BF16)
        low = (contribution - high.astype(F32)).astype(BF16)
        stacked = jnp.concatenate([high, low], axis=0)
        dense = jnp.dot(onehot[...], stacked, preferred_element_type=F32)
        for half in range(2):
            source[t, half] = dense[:, half * HALF : (half + 1) * HALF].reshape(CX, CY, HALF)

    base_step(0)

    pl.semaphore_wait(barrier, 31 + faces_half.astype(I32))

    def send_traces():
        return pltpu.make_async_remote_copy(
            src_ref=traces.at[spot, z_hi, pl.ds(0, 2)], dst_ref=traces.at[spot, z_hi, pl.ds(0, 2)],
            send_sem=zs_sem.at[0], recv_sem=zr_sem.at[0], device_id=partner, device_id_type=MESH)

    def get_traces():
        return pltpu.make_async_remote_copy(
            src_ref=traces.at[spot, 1 - z_hi, pl.ds(0, 2)], dst_ref=traces.at[spot, 1 - z_hi, pl.ds(0, 2)],
            send_sem=zs_sem.at[0], recv_sem=zr_sem.at[0], device_id=partner, device_id_type=MESH)

    def pass_traces(i):
        peer, _ = spot_peer(i)
        return pltpu.make_async_remote_copy(
            src_ref=traces.at[spot, :, pl.ds(0, 2)], dst_ref=traces.at[spot, :, pl.ds(0, 2)],
            send_sem=ts_sem.at[i], recv_sem=tr_sem.at[spot], device_id=peer, device_id_type=MESH)

    send_traces().start()
    each(sends_x, x_copy, 0, "start")
    each_y(sends_y, ALL, 0, "start")
    get_traces().wait_recv()

    def start_trace(i, carry):
        pass_traces(i).start()
        return carry

    lax.fori_loop(1, 16, start_trace, 0)

    def wait_trace(i, carry):
        peer, other = spot_peer(i)
        pltpu.make_async_remote_copy(
            src_ref=traces.at[other, :, pl.ds(0, 2)], dst_ref=traces.at[other, :, pl.ds(0, 2)],
            send_sem=ts_sem.at[i], recv_sem=tr_sem.at[other], device_id=peer, device_id_type=MESH).wait_recv()
        return carry

    lax.fori_loop(1, 16, wait_trace, 0)
    make_source(0)

    pool = (flag((iota((256, 128), 0) >> 1) == iota((256, 128), 1)) * 0.125).astype(BF16)

    def restrict(first, rows):
        pairs = []
        for half in range(2):
            planes = fine[half, pl.ds(2 * first, 2 * rows)].reshape(rows, 2, CY, HALF)
            pairs.append((planes[:, 0] + planes[:, 1]).reshape(rows * CY, HALF))
        both = jnp.concatenate(pairs, axis=1)
        high = both.astype(BF16)
        left = both - high.astype(F32)
        mid = left.astype(BF16)
        last = (left - mid.astype(F32)).astype(BF16)
        pooled[pl.ds(0, rows * CY), :] = (
            jnp.dot(high, pool, preferred_element_type=F32)
            + jnp.dot(mid, pool, preferred_element_type=F32)
            + jnp.dot(last, pool, preferred_element_type=F32))
        size = rows * CY // 2
        coarse = pooled[pl.ds(0, size, stride=2), :] + pooled[pl.ds(1, size, stride=2), :]
        local[pl.ds(first, rows)] = coarse.reshape(rows, 8, HALF)

    late = jnp.where(gx < GX // 2, CX // 2 - 2, 0)
    early = jnp.where(gx < GX // 2, 0, 2)
    OWNERS = range(4, 11)
    owns = (shot >= OWNERS[0]) & (shot <= OWNERS[-1])
    core = lax.rem(shot, 2)
    twin = {"shot": shot + 1 - 2 * core}

    def pair_of(owner):
        return pl.ds(early + 2 * (owner - OWNERS[0]), 2)

    def row_copy(owner, source_shot):
        return pltpu.make_async_remote_copy(
            src_ref=local.at[pair_of(owner)], dst_ref=arrived.at[source_shot],
            send_sem=rs_sem.at[owner], recv_sem=rr_sem.at[source_shot], device_id={"shot": owner}, device_id_type=MESH)

    def sum_copy(i, owner):
        peer, _ = shot_peer(i)
        return pltpu.make_async_remote_copy(
            src_ref=total.at[pair_of(owner)], dst_ref=total.at[pair_of(owner)],
            send_sem=as_sem.at[i], recv_sem=ar_sem.at[owner], device_id=peer, device_id_type=MESH)

    def twin_copy():
        return pltpu.make_async_remote_copy(
            src_ref=local.at[late + 1 - core], dst_ref=from_twin,
            send_sem=es_sem.at[0], recv_sem=er_sem.at[0], device_id=twin, device_id_type=MESH)

    def late_peer(i):
        return lax.rem(shot + 2 * i, SHOTS)

    def late_copy(i, source_shot):
        chip = lax.div(source_shot, 2)
        return pltpu.make_async_remote_copy(
            src_ref=late_rows.at[chip], dst_ref=late_rows.at[chip],
            send_sem=bs_sem.at[i], recv_sem=br_sem.at[chip], device_id={"shot": late_peer(i)}, device_id_type=MESH)

    def swap_copy(which):
        return pltpu.make_async_remote_copy(
            src_ref=total.at[late + which], dst_ref=total.at[late + which],
            send_sem=es_sem.at[1], recv_sem=er_sem.at[1], device_id=twin, device_id_type=MESH)

    def chips_do(make, act):
        def one(i, carry):
            getattr(make(i), act)()
            return carry

        lax.fori_loop(1, SHOTS // 2, one, 0)

    def rows_do(act):
        for owner in OWNERS:
            @pl.when(owner != shot)
            def _():
                getattr(row_copy(owner, shot), act)()

    def shots_do(make, act):
        def one(i, carry):
            getattr(make(i), act)()
            return carry

        lax.fori_loop(1, SHOTS, one, 0)

    for t in range(STEPS - 1):
        each_y(gets_y, MIDDLE, t, "wait_recv")
        if t > 0:
            fix_middle(t)
            each_y(sends_y, MIDDLE, t + 1, "start")
        each_y(gets_y, OUTER, t, "wait_recv")
        each(gets_x, x_copy, t, "wait_recv")
        fix_edges(t, LO)
        fix_edges(t, HI)
        each(sends_x, x_copy, t + 1, "start")
        each_y(sends_y, OUTER, t + 1, "start")
        if t == 0:
            fix_middle(t)
            each_y(sends_y, MIDDLE, t + 1, "start")
        make_source(t + 1)
        base_step(t + 1)

    t = STEPS - 1
    each_y(gets_y, MIDDLE, t, "wait_recv")
    fix_middle(t)
    each_y(gets_y, OUTER, t, "wait_recv")

    def edge(side):
        @pl.when(gets_x[side])
        def _():
            x_copy(t, side).wait_recv()

        fix_edges(t, side)

    lower = gx < GX // 2

    @pl.when(lower)
    def _():
        edge(LO)
        restrict(0, CX // 2 - 2)

    @pl.when(jnp.logical_not(lower))
    def _():
        edge(HI)
        restrict(2, CX // 2 - 2)

    rows_do("start")

    @pl.when(lower)
    def _():
        edge(HI)
        restrict(CX // 2 - 2, 2)

    @pl.when(jnp.logical_not(lower))
    def _():
        edge(LO)
        restrict(0, 2)

    twin_copy().start()
    twin_copy().wait_recv()
    late_rows[lax.div(shot, 2)] = local[late + core] + from_twin[...]
    chips_do(lambda i: late_copy(i, shot), "start")

    @pl.when(owns)
    def _():
        arrived[shot] = local[pair_of(shot)]
        shots_do(lambda i: row_copy(shot, shot_peer(i)[1]), "wait_recv")
        total[pair_of(shot)] = jnp.sum(arrived[...], axis=0)
        shots_do(lambda i: sum_copy(i, shot), "start")

    send_traces().wait_send()

    def end_trace(i, carry):
        pass_traces(i).wait_send()
        return carry

    lax.fori_loop(1, 16, end_trace, 0)
    for t in range(STEPS):
        each(sends_x, x_copy, t, "wait_send")
        each_y(sends_y, ALL, t, "wait_send")
    rows_do("wait_send")
    twin_copy().wait_send()
    chips_do(lambda i: late_copy(i, late_peer(i)), "wait_recv")
    total[late + core] = jnp.sum(late_rows[...], axis=0)
    swap_copy(core).start()
    for owner in OWNERS:
        @pl.when(owner != shot)
        def _():
            sum_copy(1, owner).wait_recv()
    swap_copy(1 - core).wait_recv()

    grad_o[...] = total[...]

    chips_do(lambda i: late_copy(i, shot), "wait_send")
    swap_copy(core).wait_send()

    @pl.when(owns)
    def _():
        shots_do(lambda i: sum_copy(i, shot), "wait_send")


def hand_over(prev_i, cur_i, grad_i, prev_o, cur_o, grad_o, sem):
    copies = []
    for n in range(2 * PARTS):
        src, dst = ((prev_i, prev_o), (cur_i, cur_o))[n // PARTS]
        part = pl.ds(n % PARTS * (CX // PARTS), CX // PARTS)
        copies.append(pltpu.make_async_copy(src.at[part], dst.at[part], sem.at[n]))
    copies.append(pltpu.make_async_copy(grad_i, grad_o, sem.at[2 * PARTS]))
    for copy in copies:
        copy.start()
    for copy in copies:
        copy.wait()


def local_part(adj_prev, adj_cur, fwd_accel, courant2, traces, weights, rblock, column, counts):
    tile = (CX, CY, 2 * HALF)
    any_ = pl.BlockSpec(memory_space=pl.ANY)
    vmem = pl.BlockSpec(memory_space=pltpu.VMEM)
    dma = pltpu.SemaphoreType.DMA
    results = (
        jax.ShapeDtypeStruct(tile, F32),
        jax.ShapeDtypeStruct(tile, F32),
        jax.ShapeDtypeStruct((CX // 2, CY // 2, HALF), F32),
    )
    made = pl.pallas_call(
        kernel,
        out_shape=results,
        in_specs=[any_] * 9,
        out_specs=(vmem, vmem, vmem),
        scratch_shapes=[
            pltpu.VMEM((STEPS + 1, 2, CX + 8, 32, HALF), F32),
            pltpu.VMEM((2, CX, CY, HALF), F32),
            pltpu.VMEM((STEPS, 2, CX, CY, HALF), BF16),
            pltpu.VMEM((2, CX, CY, HALF), F32),
            pltpu.VMEM((SLOTS * RB, 256), BF16),
            pltpu.VMEM((1, STEPS, 64), BF16),
            pltpu.VMEM((1, SLOTS), I32),
            pltpu.VMEM((1, SLOTS), I32),
            pltpu.VMEM((1, 1), I32),
            pltpu.VMEM((2, CX, CY, HALF), F32),
            pltpu.VMEM((STEPS, 2, CX, CY, HALF), F32),
            pltpu.VMEM((2, CX, CY, HALF), F32),
            pltpu.VMEM((CX, CY, 512), BF16),
            pltpu.VMEM((512, 256), BF16),
            pltpu.VMEM((256, 256), BF16),
            pltpu.VMEM((STEPS, 2, CX, 16, HALF), F32),
            pltpu.VMEM((STEPS, 2, CX, 16, HALF), F32),
            pltpu.VMEM((STEPS, 2, 2, 5, CY, HALF), BF16),
            pltpu.VMEM((STEPS, 2, 2, 5, CY, HALF), BF16),
            pltpu.VMEM((16, 2, 8, HALF), F32),
            pltpu.VMEM((8, HALF), F32),
            pltpu.VMEM((128, 1024), BF16),
            pltpu.VMEM((CX * CY, 2 * SLOTS), BF16),
            pltpu.VMEM((SLOTS, 32), F32),
            pltpu.VMEM((224, HALF), F32),
            pltpu.VMEM((CX // 2, 8, HALF), F32),
            pltpu.VMEM((SHOTS, 2, 8, HALF), F32),
            pltpu.VMEM((8, HALF), F32),
            pltpu.VMEM((SHOTS // 2, 8, HALF), F32),
            pltpu.VMEM((CX // 2, 8, HALF), F32),
            dma((13,)),
            dma((STEPS, 2)), dma((STEPS, 2)), dma((STEPS, 2, 3)), dma((STEPS, 2, 3)),
            dma((1,)), dma((1,)), dma((16,)), dma((16,)),
            dma((SHOTS,)), dma((SHOTS,)), dma((2,)), dma((2,)), dma((SHOTS,)), dma((SHOTS,)), dma((SHOTS,)), dma((SHOTS,)),
        ],
        compiler_params=pltpu.CompilerParams(
            collective_id=0, has_side_effects=True, vmem_limit_bytes=53760 << 10),
    )(
        adj_prev[0], adj_cur[0], fwd_accel[0], courant2, weights[0, 0].reshape(SLOTS * RB, 256),
        traces, rblock[0], column[0], counts,
    )
    previous, current, gradient = pl.pallas_call(
        hand_over,
        out_shape=results,
        in_specs=[vmem] * 3,
        out_specs=(any_,) * 3,
        scratch_shapes=[dma((2 * PARTS + 1,))],
        compiler_params=pltpu.CompilerParams(vmem_limit_bytes=16 << 20),
    )(*made)
    return previous[None], current[None], gradient


def solution(mesh):
    return jax.shard_map(
        local_part,
        mesh=mesh,
        in_specs=(
            P("shot", "gx", "gy", None),
            P("shot", "gx", "gy", None),
            P("shot", None, "gx", "gy", None),
            P("gx", "gy", None),
            P("shot", None, ("gx", "gy")),
            P("gx", "gy", None, None, None),
            P("gx", "gy", None),
            P("gx", "gy", None),
            P("gx", "gy"),
        ),
        out_specs=(P("shot", "gx", "gy", None), P("shot", "gx", "gy", None), P("gx", "gy", None)),
        check_vma=False,
    )
```
